512 devices in a mesh: pair: 32 (over x, y), row: 16 (over z, core).
Axes of the slice: x: 4, y: 8, z: 8, core: 2. Of those that a mesh axis runs over, the one named last changes fastest.
Arguments:
- activations: float32 [32768, 8192], P('row', 'pair'), may hold values from -32 to 32
Outputs:
- rotated: float32 [32768, 8192], P('row', 'pair')
The draws below stay inside these ranges and needn't reach their ends.
All inputs are finite; a program needn't handle non-finite values.
Results may differ from the reference program's by a relative error of at most 0.0003.
Values sent between devices are 32-bit elements; how exact they have to be, the bound alone decides.
No kernel may reach another device: no remote copies, remote signals or barrier semaphores. Data moves between devices by JAX's collectives and lax.ppermute only.
A program may use at most 64 MiB of HBM per device.

```python
import math
import jax
import jax.numpy as jnp
from jax import lax

BLK = 128
ROW_DEV = 2048
STEPS = 16
N_PAIR = 32
N_ROW = 16


def draw_activations(key, part):
    key = jax.random.fold_in(key, 11)
    key_cols, key_base = jax.random.split(key, 2)
    row_count = ROW_DEV * N_ROW
    col_count = 2 * BLK * N_PAIR
    col_index = jnp.arange(col_count)
    pair_index = (col_index // (2 * BLK)).astype(jnp.float32)
    lower_flag = col_index // BLK % 2
    lift = 1.0 + 0.75 * pair_index / max(N_PAIR - 1, 1)
    spread = jax.random.uniform(key_cols, (col_count,), jnp.float32)
    upper_scale = jnp.exp(spread * math.log(2.5))
    lower_scale = 0.1 * jnp.exp(spread * math.log(3.5))
    col_scale = jnp.where(lower_flag == 0, upper_scale, lower_scale) * lift
    row_lift = 1.0 + 0.7 * (jnp.arange(row_count) // ROW_DEV).astype(jnp.float32) / max(N_ROW - 1, 1)
    base = jax.random.truncated_normal(key_base, -4.0, 4.0, (row_count, col_count), jnp.float32)
    return base * row_lift[:, None] * col_scale[None, :]


def setup_inputs(seed: int = 0) -> dict:
    arg_keys = jax.random.split(jax.random.key(seed), 2)
    activations = draw_activations(jax.random.fold_in(arg_keys[1], 71), 0)
    return dict(activations=activations)


def turn_columns(matrix, cos_part, sin_part, half_size):
    upper_part = matrix[:, :half_size]
    lower_part = matrix[:, half_size:]
    return jnp.concatenate((upper_part * cos_part + lower_part * sin_part, lower_part * cos_part - upper_part * sin_part), axis=1)

def turn_rows(matrix, cos_part, sin_part, half_size):
    upper_part = matrix[:half_size, :]
    lower_part = matrix[half_size:, :]
    cos_col = cos_part[:, None]
    sin_col = sin_part[:, None]
    return jnp.concatenate((upper_part * cos_col + lower_part * sin_col, lower_part * cos_col - upper_part * sin_col), axis=0)

def roll_lower(matrix, dim_axis, half_size, offset_by):
    if dim_axis == 0:
        return jnp.concatenate((matrix[:half_size], jnp.roll(matrix[half_size:], offset_by, axis=0)), axis=0)
    return jnp.concatenate((matrix[:, :half_size], jnp.roll(matrix[:, half_size:], offset_by, axis=1)), axis=1)

def jacobi_rotations(gram_matrix, step_count):
    half_size = gram_matrix.shape[0] // 2

    def one_step(step_idx, carried):
        gram_now, rotation = carried
        diag_vals = jnp.diagonal(gram_now)
        upper_diag = diag_vals[:half_size]
        lower_diag = diag_vals[half_size:]
        coupling = jnp.diagonal(gram_now[:half_size, half_size:])
        rot_angle = 0.5 * jnp.arctan2(2.0 * coupling, upper_diag - lower_diag)
        cos_part = jnp.cos(rot_angle)
        sin_part = jnp.sin(rot_angle)
        gram_now = turn_rows(turn_columns(gram_now, cos_part, sin_part, half_size), cos_part, sin_part, half_size)
        rotation = turn_columns(rotation, cos_part, sin_part, half_size)
        gram_now = roll_lower(roll_lower(gram_now, 0, half_size, 1), 1, half_size, 1)
        rotation = roll_lower(rotation, 1, half_size, 1)
        return (gram_now, rotation)
    start = (gram_matrix, jnp.eye(gram_matrix.shape[0], dtype=gram_matrix.dtype))
    gram_end, rotation = lax.fori_loop(0, step_count, one_step, start)
    return roll_lower(rotation, 1, half_size, -step_count)

def rotate_pair(pair_cols):
    gram_matrix = jnp.dot(pair_cols.T, pair_cols, precision=lax.Precision.HIGHEST)
    rotation = jacobi_rotations(gram_matrix, STEPS)
    return jnp.dot(pair_cols, rotation, precision=lax.Precision.HIGHEST)

def reference(activations):
    row_count = activations.shape[0]
    blocks = activations.reshape(row_count, N_PAIR, 2, BLK)
    upper_cols = jnp.transpose(blocks[:, :, 0, :], (1, 0, 2))
    lower_cols = jnp.transpose(blocks[:, :, 1, :], (1, 0, 2))
    sum_squares = jnp.sum(activations * activations)
    first_out = lax.map(rotate_pair, jnp.concatenate((upper_cols, lower_cols), axis=2))
    upper_one = first_out[:, :, :BLK]
    lower_one = jnp.roll(first_out[:, :, BLK:], 1, axis=0)
    second_out = lax.map(rotate_pair, jnp.concatenate((upper_one, lower_one), axis=2))
    rms_value = jnp.sqrt(sum_squares / activations.size)
    result = second_out / rms_value
    return jnp.transpose(result, (1, 0, 2)).reshape(row_count, 2 * BLK * N_PAIR)
```

```python
import jax
import jax.numpy as jnp
from jax import lax
from jax.experimental import pallas as pl
from jax.experimental.pallas import tpu as pltpu
from jax.sharding import PartitionSpec as P

STEPS = 16
BLK = 128
BAND = 16
ROWS = 4 * BAND
TILE = 512
F32 = jnp.float32
BF16 = jnp.bfloat16


def split(value):
    high = value.astype(BF16)
    return high, (value - high.astype(F32)).astype(BF16)


def mm(left, right, dims):
    return lax.dot_general(left, right, (dims, ((), ())), preferred_element_type=F32)


def gram_tile(tile):
    high, low = split(tile)
    rows = ((0,), (0,))
    cross = mm(high, low, rows)
    return mm(high, high, rows) + mm(low, low, rows) + (cross + cross.T)


def take_band(block):
    turned = jnp.concatenate(
        [
            pltpu.roll(block[first : first + 8], (BAND - 8 - first) % BLK, 1)
            for first in range(0, BLK, 8)
        ],
        axis=0,
    )
    left = 7 - lax.broadcasted_iota(jnp.int32, (BLK, BLK), 0) % 8
    for shift in (1, 2, 4):
        turned = jnp.where(left & shift != 0, pltpu.roll(turned, shift, 1), turned)
    return turned.T[:BAND, :]


def store_bands(bands_ref, gram):
    for q in range(4):
        row, col = q // 2 * BLK, q % 2 * BLK
        band = take_band(gram[row : row + BLK, col : col + BLK])
        for k in range(BAND):
            bands_ref[BAND * q + k : BAND * q + k + 1, :] = band[BAND - 1 - k : BAND - k, :]


def put_band(band, first):
    padded = jnp.concatenate((band, jnp.zeros((BLK - BAND, BLK), F32)), axis=0)
    return pltpu.roll(padded.T, first % BLK, 1, stride=1, stride_axis=0)


def half_angle(gap, twice):
    gap_size = jnp.abs(gap)
    twice_size = jnp.abs(twice)
    largest = jnp.maximum(gap_size, twice_size)
    unit = 1.0 / jnp.where(largest > 0.0, largest, 1.0)
    gap_size = jnp.where(largest > 0.0, gap_size * unit, 1.0)
    twice_size = twice_size * unit
    inverse = lax.rsqrt(gap_size * gap_size + twice_size * twice_size)
    half = 0.5 + 0.5 * (gap_size * inverse)
    half_inverse = lax.rsqrt(half)
    large = half * half_inverse
    small = (0.5 * twice_size) * inverse * half_inverse
    sign = jnp.where(twice < 0.0, -1.0, 1.0)
    ahead = gap >= 0.0
    return jnp.where(ahead, large, small), sign * jnp.where(ahead, small, large)


def jacobi_bands(bands):
    last = BAND - 1
    uu, ul, lu, ll = (bands[BAND * i : BAND * (i + 1)] for i in range(4))
    row_ids = lax.broadcasted_iota(jnp.int32, (BAND, BLK), 0)
    is_first = row_ids == 0
    one = jnp.where(row_ids == last, 1.0, 0.0).astype(F32)
    zero = jnp.zeros((BAND, BLK), F32)
    u_top, u_low, l_top, l_low = one, zero, zero, one
    for step in range(STEPS):
        cos_row, sin_row = half_angle(uu[:1, :] - ll[:1, :], 2.0 * ul[:1, :])
        cos_c = jnp.broadcast_to(cos_row, (BAND, BLK))
        sin_c = jnp.broadcast_to(sin_row, (BAND, BLK))
        u_top, l_top = u_top * cos_c + l_top * sin_c, l_top * cos_c - u_top * sin_c
        u_low, l_low = u_low * cos_c + l_low * sin_c, l_low * cos_c - u_low * sin_c
        if step == STEPS - 1:
            break
        cos_d = pltpu.roll(cos_c, 0, 1, stride=1, stride_axis=0)
        sin_d = pltpu.roll(sin_c, 0, 1, stride=1, stride_axis=0)
        uu, lu = uu * cos_c + lu * sin_c, lu * cos_c - uu * sin_c
        ul, ll = ul * cos_c + ll * sin_c, ll * cos_c - ul * sin_c
        uu, ul = uu * cos_d + ul * sin_d, ul * cos_d - uu * sin_d
        lu, ll = lu * cos_d + ll * sin_d, ll * cos_d - lu * sin_d
        ul = pltpu.roll(ul, last, 0)
        lu = jnp.where(is_first, ul, pltpu.roll(pltpu.roll(lu, 1, 0), 1, 1))
        ll = pltpu.roll(ll, 1, 1)
        l_top = pltpu.roll(pltpu.roll(l_top, last, 0), 1, 1)
        l_low = pltpu.roll(pltpu.roll(l_low, last, 0), 1, 1)
    back = BLK - last
    return u_top, u_low, pltpu.roll(l_top, back, 1), pltpu.roll(l_low, back, 1)


def rotation_turned(bands):
    u_top, u_low, l_top, l_low = jacobi_bands(bands)
    upper = jnp.concatenate((put_band(u_top, 1 - BAND), put_band(u_low, 1 - BAND)), axis=1)
    lower = jnp.concatenate((put_band(l_top, 0), put_band(l_low, 0)), axis=1)
    return jnp.concatenate((upper, lower), axis=0)


def times_turned(tile, turned):
    high, low = split(tile)
    turned_high, turned_low = split(turned)
    last = ((1,), (1,))
    return mm(high, turned_high, last) + (mm(high, turned_low, last) + mm(low, turned_high, last))


def gram_kernel(tile_ref, bands_ref, total_ref):
    @pl.when(pl.program_id(0) == 0)
    def _():
        total_ref[...] = jnp.zeros_like(total_ref)

    total_ref[...] += gram_tile(tile_ref[...])

    @pl.when(pl.program_id(0) == pl.num_programs(0) - 1)
    def _():
        store_bands(bands_ref, total_ref[...])


def gram_bands(cols):
    rows = cols.shape[0]
    return pl.pallas_call(
        gram_kernel,
        grid=(rows // TILE,),
        in_specs=[pl.BlockSpec((TILE, 2 * BLK), lambda i: (i, 0))],
        out_specs=pl.BlockSpec((ROWS, BLK), lambda i: (0, 0)),
        out_shape=jax.ShapeDtypeStruct((ROWS, BLK), F32),
        scratch_shapes=[pltpu.VMEM((2 * BLK, 2 * BLK), F32)],
        name="gram_bands",
    )(cols)


def jacobi_kernel(bands_ref, turned_ref):
    bands = bands_ref[0]
    for i in range(1, bands_ref.shape[0]):
        bands = bands + bands_ref[i]
    turned_ref[...] = rotation_turned(bands)


def jacobi(parts):
    return pl.pallas_call(
        jacobi_kernel,
        out_shape=jax.ShapeDtypeStruct((2 * BLK, 2 * BLK), F32),
        name="jacobi",
    )(parts)


def rotate_kernel(tile_ref, turned_ref, out_ref):
    out_ref[...] = times_turned(tile_ref[...], turned_ref[...])


def rotate(cols, turned):
    rows = cols.shape[0]
    return pl.pallas_call(
        rotate_kernel,
        grid=(rows // TILE,),
        in_specs=[
            pl.BlockSpec((TILE, 2 * BLK), lambda i: (i, 0)),
            pl.BlockSpec((2 * BLK, 2 * BLK), lambda i: (0, 0)),
        ],
        out_specs=pl.BlockSpec((TILE, 2 * BLK), lambda i: (i, 0)),
        out_shape=jax.ShapeDtypeStruct(cols.shape, F32),
        name="rotate",
    )(cols, turned)


def passed_along(value, axis, steps):
    count = lax.axis_size(axis)
    pairs = [(source, (source + steps) % count) for source in range(count)]
    return lax.ppermute(value, axis, pairs)


def to_all(value, axis):
    count = lax.axis_size(axis)
    copies = jnp.broadcast_to(value[None], (count,) + value.shape)
    return lax.all_to_all(copies, axis, 0, 0, tiled=True)


def body(activations):
    entry_count = (
        activations.shape[0] * activations.shape[1] * lax.axis_size("pair") * lax.axis_size("row")
    )
    parts_one = lax.all_gather(gram_bands(activations), "row")
    rotated_one = rotate(activations, jacobi(parts_one))
    arrived = passed_along(rotated_one[:, BLK:], "pair", 1)
    diagonals = jnp.sum(parts_one[:, 0] + parts_one[:, 3 * BAND], axis=0)
    diagonals = lax.optimization_barrier((diagonals, rotated_one[:1, :1]))[0]
    sum_squares = jnp.sum(to_all(diagonals.reshape(1, BLK), "pair"))
    rms_value = jnp.sqrt(sum_squares / entry_count)
    pair_two = jnp.concatenate((rotated_one[:, :BLK], arrived), axis=1)
    parts_two = lax.all_gather(gram_bands(pair_two), "row")
    return rotate(pair_two, jacobi(parts_two) / rms_value)


def solution(mesh):
    return jax.shard_map(
        body,
        mesh=mesh,
        in_specs=(P("row", "pair"),),
        out_specs=P("row", "pair"),
        check_vma=False,
    )
```

```python
import functools

import jax
import jax.numpy as jnp
from jax import lax
from jax.experimental import pallas as pl
from jax.experimental.pallas import tpu as pltpu
from jax.sharding import PartitionSpec as P

STEPS = 16
BLK = 128
BAND = 16
WIDE = 2 * BAND
TILE = 1024
LIMIT = 40 << 20
COST = pl.CostEstimate(flops=2_000_000_000, bytes_accessed=6_000_000, transcendentals=0)
F32 = jnp.float32
BF16 = jnp.bfloat16


def split(value):
    high = value.astype(BF16)
    return high, (value - high.astype(F32)).astype(BF16)


def mm(left, right, dims):
    return lax.dot_general(left, right, (dims, ((), ())), preferred_element_type=F32)


def gram_tile(tile):
    high, low = split(tile)
    rows = ((0,), (0,))
    cross = mm(high, low, rows)
    return mm(high, high, rows) + mm(low, low, rows) + (cross + cross.T)


def take_band(block, width):
    turned = jnp.concatenate(
        [
            pltpu.roll(block[first : first + 8], (width - 8 - first) % BLK, 1)
            for first in range(0, BLK, 8)
        ],
        axis=0,
    )
    left = 7 - lax.broadcasted_iota(jnp.int32, (BLK, BLK), 0) % 8
    for shift in (1, 2, 4):
        turned = jnp.where(left & shift != 0, pltpu.roll(turned, shift, 1), turned)
    return turned.T[:width, :]


def bands_of(block, width):
    band = take_band(block, width)
    return [band[width - 1 - k : width - k, :] for k in range(width)]


def put_band(band, first):
    padded = jnp.concatenate((band, jnp.zeros((BLK - BAND, BLK), F32)), axis=0)
    return pltpu.roll(padded.T, first % BLK, 1, stride=1, stride_axis=0)


def half_angle(gap, twice):
    gap_size = jnp.abs(gap)
    twice_size = jnp.abs(twice)
    largest = jnp.maximum(gap_size, twice_size)
    scale = jnp.where(largest < 2.0**-20, 2.0**80, 1.0)
    gap_size = jnp.where(largest > 0.0, gap_size * scale, 1.0)
    twice_size = twice_size * scale
    inverse = lax.rsqrt(gap_size * gap_size + twice_size * twice_size)
    half = 0.5 + (0.5 * gap_size) * inverse
    half_inverse = lax.rsqrt(half)
    large = half * half_inverse
    small = (0.5 * twice_size) * inverse * half_inverse
    sign = jnp.where(twice < 0.0, -1.0, 1.0)
    ahead = gap >= 0.0
    return jnp.where(ahead, large, small), sign * jnp.where(ahead, small, large)


def row_copies(rows, index):
    return jnp.broadcast_to(rows[index : index + 1, :], (8, BLK))


def ahead_by_one(rows):
    return pltpu.roll(rows, 1, 1)


def jacobi_bands(uu, ul, lu, ll):
    count = uu.shape[0]
    last = BAND - 1
    is_first = lax.broadcasted_iota(jnp.int32, (count, BLK), 0) == 0
    row_ids = lax.broadcasted_iota(jnp.int32, (BAND, BLK), 0)
    one = jnp.where(row_ids == last, 1.0, 0.0).astype(F32)
    zero = jnp.zeros((BAND, BLK), F32)
    u_top, u_low, l_top, l_low = one, zero, zero, one
    u_diag, l_diag, coupling = row_copies(uu, 0), row_copies(ll, 0), row_copies(ul, 0)
    for step in range(STEPS):
        cos, sin = half_angle(u_diag - l_diag, 2.0 * coupling)
        final_step = step == STEPS - 1
        if not final_step:
            u_past, l_past, x_past = (ahead_by_one(v) for v in (u_diag, l_diag, coupling))
            cos_past, sin_past = ahead_by_one(cos), ahead_by_one(sin)
            u_diag, coupling = (
                cos * (cos * u_diag + sin * coupling) + sin * (cos * coupling + sin * l_diag),
                cos_past * (cos * row_copies(ul, 1) + sin * row_copies(ll, 1))
                - sin_past * (cos * row_copies(uu, 1) + sin * row_copies(lu, 1)),
            )
            l_diag = cos_past * (cos_past * l_past - sin_past * x_past) - sin_past * (
                cos_past * x_past - sin_past * u_past
            )
        cos_b = jnp.concatenate([cos] * (BAND // 8), axis=0)
        sin_b = jnp.concatenate([sin] * (BAND // 8), axis=0)
        u_top, l_top = u_top * cos_b + l_top * sin_b, l_top * cos_b - u_top * sin_b
        u_low, l_low = u_low * cos_b + l_low * sin_b, l_low * cos_b - u_low * sin_b
        if final_step and count == BAND:
            break
        cos_c = jnp.concatenate([cos] * (count // 8), axis=0)
        sin_c = jnp.concatenate([sin] * (count // 8), axis=0)
        cos_d = jnp.concatenate(
            [pltpu.roll(cos, 8 * i, 1, stride=1, stride_axis=0) for i in range(count // 8)], axis=0
        )
        sin_d = jnp.concatenate(
            [pltpu.roll(sin, 8 * i, 1, stride=1, stride_axis=0) for i in range(count // 8)], axis=0
        )
        uu, lu = uu * cos_c + lu * sin_c, lu * cos_c - uu * sin_c
        ul, ll = ul * cos_c + ll * sin_c, ll * cos_c - ul * sin_c
        uu, ul = uu * cos_d + ul * sin_d, ul * cos_d - uu * sin_d
        lu, ll = lu * cos_d + ll * sin_d, ll * cos_d - lu * sin_d
        if final_step:
            break
        ul = pltpu.roll(ul, count - 1, 0)
        lu = jnp.where(is_first, ul, ahead_by_one(pltpu.roll(lu, 1, 0)))
        ll = ahead_by_one(ll)
        l_top = ahead_by_one(pltpu.roll(l_top, last, 0))
        l_low = ahead_by_one(pltpu.roll(l_low, last, 0))
    back = BLK - last
    l_top, l_low = pltpu.roll(l_top, back, 1), pltpu.roll(l_low, back, 1)
    return u_top, u_low, l_top, l_low, uu[:BAND], pltpu.roll(ll[:BAND], back, 1)


def turned_half(top, low, first):
    return jnp.concatenate((put_band(top, first), put_band(low, first)), axis=1)


def times_turned(tile, turned):
    high, low = split(tile)
    turned_high, turned_low = split(turned)
    last = ((1,), (1,))
    return mm(high, turned_high, last) + (mm(high, turned_low, last) + mm(low, turned_high, last))


def summed(parts_ref, first=0, step=1):
    total = parts_ref[first]
    for i in range(first + step, parts_ref.shape[0], step):
        total = total + parts_ref[i]
    return total


def jacobi_kernel(core_ref, parts_ref, turned_ref, sent_ref, kept_ref):
    upper, lower = summed(parts_ref, 0, 2), summed(parts_ref, 1, 2)
    u_top, u_low, l_top, l_low, uu, ll = jacobi_bands(
        upper[:WIDE], upper[WIDE:], lower[:WIDE], lower[WIDE:]
    )
    first_core = core_ref[0] == 0
    sent_ref[:BAND, :] = jnp.where(first_core, l_top, u_top)
    sent_ref[BAND : 2 * BAND, :] = jnp.where(first_core, l_low, u_low)
    sent_ref[2 * BAND :, :] = jnp.where(first_core, ll, uu)
    kept_ref[...] = jnp.where(first_core, uu, ll)
    turned_ref[:BLK, :] = turned_half(u_top, u_low, 1 - BAND)
    turned_ref[BLK:, :] = turned_half(l_top, l_low, 0)


def jacobi(core, parts):
    return pl.pallas_call(
        jacobi_kernel,
        in_specs=[
            pl.BlockSpec(memory_space=pltpu.SMEM),
            pl.BlockSpec(memory_space=pltpu.VMEM),
        ],
        out_shape=(
            jax.ShapeDtypeStruct((2 * BLK, 2 * BLK), F32),
            jax.ShapeDtypeStruct((3 * BAND, BLK), F32),
            jax.ShapeDtypeStruct((BAND, BLK), F32),
        ),
        name="jacobi",
    )(core, parts)


def rotate_kernel(tile_ref, turned_ref, upper_ref, lower_ref):
    out = times_turned(tile_ref[...], turned_ref[...])
    upper_ref[...] = out[:, :BLK]
    lower_ref[...] = out[:, BLK:]


def rotate(cols, turned):
    rows = cols.shape[0]
    half = jax.ShapeDtypeStruct((rows, BLK), F32)
    half_spec = pl.BlockSpec((TILE, BLK), lambda i: (i, 0))
    return pl.pallas_call(
        rotate_kernel,
        grid=(rows // TILE,),
        in_specs=[
            pl.BlockSpec((TILE, 2 * BLK), lambda i: (i, 0)),
            pl.BlockSpec((2 * BLK, 2 * BLK), lambda i: (0, 0)),
        ],
        out_specs=(half_spec, half_spec),
        out_shape=(half, half),
        compiler_params=pltpu.CompilerParams(vmem_limit_bytes=LIMIT),
        cost_estimate=COST,
        name="rotate",
    )(cols, turned)


def cross_tile(left, right):
    left_high, left_low = split(left)
    right_high, right_low = split(right)
    rows = ((0,), (0,))
    return (
        mm(left_high, right_high, rows)
        + mm(left_low, right_low, rows)
        + (mm(left_high, right_low, rows) + mm(left_low, right_high, rows))
    )


def link_kernel(
    core_ref, raw_ref, got_ref, kept_ref, traces_ref, upper_ref, lower_ref,
    other_ref, bands_ref, diag_ref, turned_ref, total_ref,
):
    first_core = core_ref[0] == 0

    @pl.when(pl.program_id(0) == 0)
    def _():
        got = got_ref[...]
        top, low = got[:BAND], got[BAND : 2 * BAND]

        @pl.when(first_core)
        def _():
            turned_ref[...] = turned_half(top, low, 0)
            diag_ref[:BAND, :] = kept_ref[...]
            diag_ref[BAND:, :] = got[2 * BAND :]

        @pl.when(jnp.logical_not(first_core))
        def _():
            turned_ref[...] = turned_half(top, low, 1 - BAND)
            diag_ref[:BAND, :] = got[2 * BAND :]
            diag_ref[BAND:, :] = kept_ref[...]

        total_ref[...] = jnp.zeros_like(total_ref)

    other = times_turned(raw_ref[...], turned_ref[...])
    other_ref[...] = other
    left = jnp.where(first_core, upper_ref[...], other)
    right = jnp.where(first_core, other, lower_ref[...])
    total_ref[...] += cross_tile(left, right)

    @pl.when(pl.program_id(0) == pl.num_programs(0) - 1)
    def _():
        cross = total_ref[...]
        bands = jnp.concatenate(
            bands_of(cross, BAND) + [summed(traces_ref)] + bands_of(cross.T, BAND)[1:], axis=0
        )
        for i in range(bands_ref.shape[0]):
            bands_ref[i] = bands


def link(core, raw, got, kept, traces, upper, lower, copies):
    rows = raw.shape[0]
    half_spec = pl.BlockSpec((TILE, BLK), lambda i: (i, 0))
    return pl.pallas_call(
        link_kernel,
        grid=(rows // TILE,),
        in_specs=[
            pl.BlockSpec(memory_space=pltpu.SMEM),
            pl.BlockSpec((TILE, 2 * BLK), lambda i: (i, 0)),
            pl.BlockSpec((3 * BAND, BLK), lambda i: (0, 0)),
            pl.BlockSpec((BAND, BLK), lambda i: (0, 0)),
            pl.BlockSpec(traces.shape, lambda i: (0, 0, 0)),
            half_spec,
            half_spec,
        ],
        out_specs=(
            half_spec,
            pl.BlockSpec((copies, 2 * BAND, BLK), lambda i: (0, 0, 0)),
            pl.BlockSpec((2 * BAND, BLK), lambda i: (0, 0)),
        ),
        out_shape=(
            jax.ShapeDtypeStruct((rows, BLK), F32),
            jax.ShapeDtypeStruct((copies, 2 * BAND, BLK), F32),
            jax.ShapeDtypeStruct((2 * BAND, BLK), F32),
        ),
        scratch_shapes=[pltpu.VMEM((BLK, 2 * BLK), F32), pltpu.VMEM((BLK, BLK), F32)],
        compiler_params=pltpu.CompilerParams(vmem_limit_bytes=LIMIT),
        name="link",
    )(core, raw, got, kept, traces, upper, lower)


def final_kernel(
    entry_count, core_ref, bands_ref, upper_ref, other_ref, came_ref, out_ref, turned_ref
):
    @pl.when(pl.program_id(0) == 0)
    def _():
        ul, lu, uu, ll = (bands_ref[BAND * i : BAND * (i + 1), :] for i in range(4))
        rms = jnp.sqrt(jnp.sum(lu[:1], axis=1, keepdims=True) / entry_count)
        lu = jnp.concatenate((ul[:1], lu[1:]), axis=0)
        u_top, u_low, l_top, l_low, _, _ = jacobi_bands(uu, ul, lu, ll)
        turned_ref[:BLK, :] = turned_half(u_top, u_low, 1 - BAND) / rms
        turned_ref[BLK:, :] = turned_half(l_top, l_low, 0) / rms

    lower = jnp.where(core_ref[0] == 0, other_ref[...], came_ref[...])
    pair = jnp.concatenate((upper_ref[...], lower), axis=1)
    out_ref[...] = times_turned(pair, turned_ref[...])


def final(entry_count, core, bands, upper, other, came):
    rows = upper.shape[0]
    half_spec = pl.BlockSpec((TILE, BLK), lambda i: (i, 0))
    return pl.pallas_call(
        functools.partial(final_kernel, entry_count),
        grid=(rows // TILE,),
        in_specs=[
            pl.BlockSpec(memory_space=pltpu.SMEM),
            pl.BlockSpec((4 * BAND, BLK), lambda i: (0, 0)),
            half_spec,
            half_spec,
            half_spec,
        ],
        out_specs=pl.BlockSpec((TILE, 2 * BLK), lambda i: (i, 0)),
        out_shape=jax.ShapeDtypeStruct((rows, 2 * BLK), F32),
        scratch_shapes=[pltpu.VMEM((2 * BLK, 2 * BLK), F32)],
        compiler_params=pltpu.CompilerParams(vmem_limit_bytes=LIMIT),
        name="final",
    )(core, bands, upper, other, came)


def gram_kernel(core_ref, tile_ref, bands_ref, trace_ref, total_ref):
    @pl.when(pl.program_id(0) == 0)
    def _():
        total_ref[...] = jnp.zeros_like(total_ref)

    total_ref[...] += gram_tile(tile_ref[...])

    @pl.when(pl.program_id(0) == pl.num_programs(0) - 1)
    def _():
        gram = total_ref[...]
        halves = []
        for row in (0, BLK):
            upper = bands_of(gram[row : row + BLK, :BLK], WIDE)
            lower = bands_of(gram[row : row + BLK, BLK:], WIDE)
            halves.append(jnp.concatenate(upper + lower, axis=0))
        core = core_ref[0]
        bands_ref[core] = halves[0]
        bands_ref[1 - core] = halves[1]
        trace_ref[...] = jnp.broadcast_to(
            (halves[0][:1] + halves[1][WIDE : WIDE + 1])[None], trace_ref.shape
        )


def gram_bands(core, cols, copies):
    rows = cols.shape[0]
    return pl.pallas_call(
        gram_kernel,
        grid=(rows // TILE,),
        in_specs=[
            pl.BlockSpec(memory_space=pltpu.SMEM),
            pl.BlockSpec((TILE, 2 * BLK), lambda i: (i, 0)),
        ],
        out_specs=(
            pl.BlockSpec((2, 2 * WIDE, BLK), lambda i: (0, 0, 0)),
            pl.BlockSpec((copies, 1, BLK), lambda i: (0, 0, 0)),
        ),
        out_shape=(
            jax.ShapeDtypeStruct((2, 2 * WIDE, BLK), F32),
            jax.ShapeDtypeStruct((copies, 1, BLK), F32),
        ),
        scratch_shapes=[pltpu.VMEM((2 * BLK, 2 * BLK), F32)],
        compiler_params=pltpu.CompilerParams(vmem_limit_bytes=LIMIT),
        name="gram_bands",
    )(core, cols)


class Ring:
    def __init__(self, pairs, rows):
        self.pairs, self.rows = pairs, rows

    def at(self, pair, row):
        return pair % self.pairs * self.rows + row

    def moves(self, cores, steps):
        return [
            (self.at(pair, row), self.at(pair + steps, row))
            for pair in range(self.pairs)
            for row in range(self.rows)
            if row % 2 in cores
        ]

    def swapped(self):
        return self.moves((0,), 1) + self.moves((1,), -1)

    def to_second_core(self):
        return [
            (self.at(pair, row), self.at(pair, row + 1))
            for pair in range(self.pairs)
            for row in range(0, self.rows, 2)
        ]

    def to_other_core(self):
        return [(at, at ^ 1) for at in range(self.pairs * self.rows)]

    def links(self):
        return [
            [self.at(pair, row) for row in range(0, self.rows, 2)]
            + [self.at(pair - 1, row) for row in range(1, self.rows, 2)]
            for pair in range(self.pairs)
        ]


AXES = ("pair", "row")


def body(activations):
    pairs, rows = lax.axis_size("pair"), lax.axis_size("row")
    ring = Ring(pairs, rows)
    entry_count = activations.shape[0] * activations.shape[1] * pairs * rows
    core = (lax.axis_index("row") % 2).astype(jnp.int32).reshape(1)

    raw = lax.ppermute(activations, AXES, ring.swapped())
    bands, traces = gram_bands(core, activations, pairs)
    traces = lax.all_to_all(traces, "pair", 0, 0, tiled=True)
    bands = bands[0] + lax.ppermute(bands[1], AXES, ring.to_other_core())
    turned, sent, kept = jacobi(core, lax.all_gather(bands, "row"))
    got = lax.ppermute(sent, AXES, ring.swapped())
    upper, lower = rotate(activations, turned)
    other, bands, diag = link(core, raw, got, kept, traces, upper, lower, rows)
    lower, bands = lax.optimization_barrier((lower, bands))
    came = lax.ppermute(lower, AXES, ring.moves((1,), 1))
    parts = lax.all_to_all(bands, AXES, 0, 0, axis_index_groups=ring.links(), tiled=True)
    bands = jnp.concatenate((jnp.sum(parts, axis=0), diag), axis=0)
    arrived = lax.ppermute(bands, AXES, ring.to_second_core())
    bands = jnp.where(core[0] == 0, bands, arrived)
    return final(float(entry_count), core, bands, upper, other, came)


def solution(mesh):
    return jax.shard_map(
        body,
        mesh=mesh,
        in_specs=(P("row", "pair"),),
        out_specs=P("row", "pair"),
        check_vma=False,
    )
```

```python
import functools

import jax
import jax.numpy as jnp
from jax import lax
from jax.experimental import pallas as pl
from jax.experimental.pallas import tpu as pltpu
from jax.sharding import PartitionSpec as P

STEPS = 16
BLK = 128
BAND = 16
ROWS = 4 * BAND
TILE = 1024
EARLY = 1216
LIMIT = 24 << 20
COST = pl.CostEstimate(flops=2_000_000_000, bytes_accessed=6_000_000, transcendentals=0)
F32 = jnp.float32
BF16 = jnp.bfloat16


def split(value):
    high = value.astype(BF16)
    return high, (value - high.astype(F32)).astype(BF16)


def mm(left, right, dims):
    return lax.dot_general(left, right, (dims, ((), ())), preferred_element_type=F32)


def gram_tile(tile):
    high, low = split(tile)
    rows = ((0,), (0,))
    cross = mm(high, low, rows)
    return mm(high, high, rows) + mm(low, low, rows) + (cross + cross.T)


def take_band(block, width):
    turned = jnp.concatenate(
        [
            pltpu.roll(block[first : first + 8], (width - 8 - first) % BLK, 1)
            for first in range(0, BLK, 8)
        ],
        axis=0,
    )
    left = 7 - lax.broadcasted_iota(jnp.int32, (BLK, BLK), 0) % 8
    for shift in (1, 2, 4):
        turned = jnp.where(left & shift != 0, pltpu.roll(turned, shift, 1), turned)
    return turned.T[:width, :]


def bands_of(block, width):
    band = take_band(block, width)
    return [band[width - 1 - k : width - k, :] for k in range(width)]


def put_band(band, first):
    padded = jnp.concatenate((band, jnp.zeros((BLK - BAND, BLK), F32)), axis=0)
    return pltpu.roll(padded.T, first % BLK, 1, stride=1, stride_axis=0)


def half_angle(gap, twice):
    gap_size = jnp.abs(gap)
    twice_size = jnp.abs(twice)
    largest = jnp.maximum(gap_size, twice_size)
    scale = jnp.where(largest < 2.0**-20, 2.0**80, 1.0)
    gap_size = jnp.where(largest > 0.0, gap_size * scale, 1.0)
    twice_size = twice_size * scale
    inverse = lax.rsqrt(gap_size * gap_size + twice_size * twice_size)
    half = 0.5 + (0.5 * gap_size) * inverse
    half_inverse = lax.rsqrt(half)
    large = half * half_inverse
    small = (0.5 * twice_size) * inverse * half_inverse
    sign = jnp.where(twice < 0.0, -1.0, 1.0)
    ahead = gap >= 0.0
    return jnp.where(ahead, large, small), sign * jnp.where(ahead, small, large)


def row_copies(rows, index):
    return jnp.broadcast_to(rows[index : index + 1, :], (8, BLK))


def ahead_by_one(rows):
    return pltpu.roll(rows, 1, 1)


def jacobi_bands(uu, ul, lu, ll):
    last = BAND - 1
    is_first = lax.broadcasted_iota(jnp.int32, (BAND, BLK), 0) == 0
    row_ids = lax.broadcasted_iota(jnp.int32, (BAND, BLK), 0)
    one = jnp.where(row_ids == last, 1.0, 0.0).astype(F32)
    zero = jnp.zeros((BAND, BLK), F32)
    u_top, u_low, l_top, l_low = one, zero, zero, one
    u_diag, l_diag, coupling = row_copies(uu, 0), row_copies(ll, 0), row_copies(ul, 0)
    for step in range(STEPS):
        cos, sin = half_angle(u_diag - l_diag, 2.0 * coupling)
        final_step = step == STEPS - 1
        if not final_step:
            u_past, l_past, x_past = (ahead_by_one(v) for v in (u_diag, l_diag, coupling))
            cos_past, sin_past = ahead_by_one(cos), ahead_by_one(sin)
            u_diag, coupling = (
                cos * (cos * u_diag + sin * coupling) + sin * (cos * coupling + sin * l_diag),
                cos_past * (cos * row_copies(ul, 1) + sin * row_copies(ll, 1))
                - sin_past * (cos * row_copies(uu, 1) + sin * row_copies(lu, 1)),
            )
            l_diag = cos_past * (cos_past * l_past - sin_past * x_past) - sin_past * (
                cos_past * x_past - sin_past * u_past
            )
        cos_b = jnp.concatenate([cos] * (BAND // 8), axis=0)
        sin_b = jnp.concatenate([sin] * (BAND // 8), axis=0)
        u_top, l_top = u_top * cos_b + l_top * sin_b, l_top * cos_b - u_top * sin_b
        u_low, l_low = u_low * cos_b + l_low * sin_b, l_low * cos_b - u_low * sin_b
        if final_step:
            break
        cos_d = jnp.concatenate(
            [pltpu.roll(cos, 8 * i, 1, stride=1, stride_axis=0) for i in range(BAND // 8)], axis=0
        )
        sin_d = jnp.concatenate(
            [pltpu.roll(sin, 8 * i, 1, stride=1, stride_axis=0) for i in range(BAND // 8)], axis=0
        )
        uu, lu = uu * cos_b + lu * sin_b, lu * cos_b - uu * sin_b
        ul, ll = ul * cos_b + ll * sin_b, ll * cos_b - ul * sin_b
        uu, ul = uu * cos_d + ul * sin_d, ul * cos_d - uu * sin_d
        lu, ll = lu * cos_d + ll * sin_d, ll * cos_d - lu * sin_d
        ul = pltpu.roll(ul, last, 0)
        lu = jnp.where(is_first, ul, ahead_by_one(pltpu.roll(lu, 1, 0)))
        ll = ahead_by_one(ll)
        l_top = ahead_by_one(pltpu.roll(l_top, last, 0))
        l_low = ahead_by_one(pltpu.roll(l_low, last, 0))
    back = BLK - last
    l_top, l_low = pltpu.roll(l_top, back, 1), pltpu.roll(l_low, back, 1)
    return u_top, u_low, l_top, l_low


def turned_half(top, low, first):
    return jnp.concatenate((put_band(top, first), put_band(low, first)), axis=1)


def times_turned(tile, turned):
    high, low = split(tile)
    turned_high, turned_low = split(turned)
    last = ((1,), (1,))
    return mm(high, turned_high, last) + (mm(high, turned_low, last) + mm(low, turned_high, last))


def all_bands(gram):
    rows = []
    for top in (0, BLK):
        for left in (0, BLK):
            rows += bands_of(gram[top : top + BLK, left : left + BLK], BAND)
    return jnp.concatenate(rows, axis=0)


def summed(parts_ref):
    total = parts_ref[0]
    for i in range(1, parts_ref.shape[0]):
        total = total + parts_ref[i]
    return total


def blocks(bands):
    return [bands[BAND * i : BAND * (i + 1)] for i in range(4)]


VMEM_SPEC = pl.BlockSpec(memory_space=pltpu.VMEM)
PARAMS = pltpu.CompilerParams(vmem_limit_bytes=LIMIT)


def gram_kernel(cols_ref, bands_ref, early_ref, sem):
    copy = pltpu.make_async_copy(cols_ref.at[pl.ds(0, EARLY)], early_ref, sem)
    copy.start()
    bands_ref[...] = all_bands(gram_tile(cols_ref[...]))
    copy.wait()


def gram_bands(cols):
    return pl.pallas_call(
        gram_kernel,
        in_specs=[VMEM_SPEC],
        out_specs=(VMEM_SPEC, pl.BlockSpec(memory_space=pltpu.HBM)),
        out_shape=(
            jax.ShapeDtypeStruct((ROWS, BLK), F32),
            jax.ShapeDtypeStruct((EARLY, 2 * BLK), F32),
        ),
        scratch_shapes=[pltpu.SemaphoreType.DMA(())],
        compiler_params=PARAMS,
        name="gram_bands",
    )(cols)


def jacobi_kernel(parts_ref, own_ref, trace_ref):
    bands = summed(parts_ref)
    uu, ul, lu, ll = blocks(bands)
    trace_ref[...] = jnp.broadcast_to((uu[:1] + ll[:1])[None], trace_ref.shape)
    own_ref[...] = jnp.concatenate(jacobi_bands(uu, ul, lu, ll), axis=0)


def jacobi(parts, copies):
    return pl.pallas_call(
        jacobi_kernel,
        in_specs=[VMEM_SPEC],
        out_shape=(
            pltpu.VMEM((ROWS, BLK), F32),
            jax.ShapeDtypeStruct((copies, 1, BLK), F32),
        ),
        name="jacobi",
    )(parts)


def own_kernel(cols_ref, own_ref, upper_ref, late_ref):
    u_top, u_low, l_top, l_low = blocks(own_ref[...])
    late_ref[: 2 * BAND, :] = own_ref[2 * BAND :, :]
    late_ref[2 * BAND :, :] = times_turned(cols_ref[EARLY:, :], turned_half(l_top, l_low, 0))
    upper_ref[...] = times_turned(cols_ref[...], turned_half(u_top, u_low, 1 - BAND))


def own_halves(cols, own):
    rows = cols.shape[0]
    return pl.pallas_call(
        own_kernel,
        in_specs=[VMEM_SPEC, VMEM_SPEC],
        out_shape=(
            jax.ShapeDtypeStruct((rows, BLK), F32),
            jax.ShapeDtypeStruct((2 * BAND + rows - EARLY, BLK), F32),
        ),
        cost_estimate=COST,
        compiler_params=PARAMS,
        name="own_halves",
    )(cols, own)


def link_kernel(raw_ref, late_ref, upper_ref, lower_ref, bands_ref, turned_ref, total_ref):
    step = pl.program_id(0)

    @pl.when(step == 0)
    def _():
        turned_ref[...] = turned_half(late_ref[:BAND, :], late_ref[BAND : 2 * BAND, :], 0)
        total_ref[...] = jnp.zeros_like(total_ref)

    tile = raw_ref.shape[0]
    rows = pl.ds(pl.multiple_of(step * tile, 8), tile)
    lower = times_turned(raw_ref[...], turned_ref[...])
    lower_ref[rows, :] = lower
    total_ref[...] += gram_tile(jnp.concatenate((upper_ref[rows, :], lower), axis=1))

    @pl.when(step == pl.num_programs(0) - 1)
    def _():
        late = late_ref[2 * BAND :, :]
        lower_ref[EARLY:, :] = late
        gram = gram_tile(jnp.concatenate((upper_ref[EARLY:, :], late), axis=1))
        bands_ref[...] = all_bands(total_ref[...] + gram)


def link(raw, late, upper):
    rows = upper.shape[0]
    return pl.pallas_call(
        link_kernel,
        grid=(2,),
        in_specs=[
            pl.BlockSpec((EARLY // 2, 2 * BLK), lambda i: (i, 0)),
            pl.BlockSpec(late.shape, lambda i: (0, 0)),
            pl.BlockSpec(upper.shape, lambda i: (0, 0)),
        ],
        out_specs=(
            pl.BlockSpec((rows, BLK), lambda i: (0, 0)),
            pl.BlockSpec((ROWS, BLK), lambda i: (0, 0)),
        ),
        out_shape=(
            jax.ShapeDtypeStruct((rows, BLK), F32),
            jax.ShapeDtypeStruct((ROWS, BLK), F32),
        ),
        scratch_shapes=[pltpu.VMEM((BLK, 2 * BLK), F32), pltpu.VMEM((2 * BLK, 2 * BLK), F32)],
        cost_estimate=COST,
        compiler_params=PARAMS,
        name="link",
    )(raw, late, upper)


def final_kernel(entry_count, parts_ref, traces_ref, upper_ref, lower_ref, out_ref, turned_ref):
    @pl.when(pl.program_id(0) == 0)
    def _():
        rms = jnp.sqrt(jnp.sum(summed(traces_ref), axis=1, keepdims=True) / entry_count)
        u_top, u_low, l_top, l_low = jacobi_bands(*blocks(summed(parts_ref)))
        turned_ref[:BLK, :] = turned_half(u_top, u_low, 1 - BAND) / rms
        turned_ref[BLK:, :] = turned_half(l_top, l_low, 0) / rms

    pair = jnp.concatenate((upper_ref[...], lower_ref[...]), axis=1)
    out_ref[...] = times_turned(pair, turned_ref[...])


def final(entry_count, parts, traces, upper, lower):
    rows = upper.shape[0]
    half_spec = pl.BlockSpec((TILE, BLK), lambda i: (i, 0))
    return pl.pallas_call(
        functools.partial(final_kernel, entry_count),
        grid=(rows // TILE,),
        in_specs=[
            pl.BlockSpec(parts.shape, lambda i: (0, 0, 0)),
            pl.BlockSpec(traces.shape, lambda i: (0, 0, 0)),
            half_spec,
            half_spec,
        ],
        out_specs=pl.BlockSpec((TILE, 2 * BLK), lambda i: (i, 0)),
        out_shape=jax.ShapeDtypeStruct((rows, 2 * BLK), F32),
        scratch_shapes=[pltpu.VMEM((2 * BLK, 2 * BLK), F32)],
        compiler_params=PARAMS,
        name="final",
    )(parts, traces, upper, lower)


def to_next(value):
    count = lax.axis_size("pair")
    return lax.ppermute(value, "pair", [(pair, (pair + 1) % count) for pair in range(count)])


def body(activations):
    pairs, rows = lax.axis_size("pair"), lax.axis_size("row")
    entry_count = activations.shape[0] * activations.shape[1] * pairs * rows

    bands, early = gram_bands(activations)
    raw = to_next(early)
    own, traces = jacobi(lax.all_gather(bands, "row"), pairs)
    upper, late = own_halves(activations, own)
    late = to_next(late)
    traces = lax.all_to_all(traces, "pair", 0, 0, tiled=True)
    lower, bands = link(raw, late, upper)
    bands, traces = lax.optimization_barrier((bands, traces))
    parts = lax.all_gather(bands, "row")
    return final(float(entry_count), parts, traces, upper, lower)


def solution(mesh):
    return jax.shard_map(
        body,
        mesh=mesh,
        in_specs=(P("row", "pair"),),
        out_specs=P("row", "pair"),
        check_vma=False,
    )
```

```python
import functools

import jax
import jax.numpy as jnp
from jax import lax
from jax.experimental import pallas as pl
from jax.experimental.pallas import tpu as pltpu
from jax.sharding import PartitionSpec as P

STEPS = 16
BLK = 128
BAND = 16
ROWS = 4 * BAND
TILE = 1024
EARLY = 1152
PART = 512
LIMIT = 24 << 20
COST = pl.CostEstimate(flops=2_000_000_000, bytes_accessed=6_000_000, transcendentals=0)
F32 = jnp.float32
BF16 = jnp.bfloat16


def split(value):
    high = value.astype(BF16)
    return high, (value - high.astype(F32)).astype(BF16)


def mm(left, right, dims):
    return lax.dot_general(left, right, (dims, ((), ())), preferred_element_type=F32)


def gram_tile(tile):
    high, low = split(tile)
    rows = ((0,), (0,))
    cross = mm(high, low, rows)
    return mm(high, high, rows) + mm(low, low, rows) + (cross + cross.T)


def take_band(block, width):
    turned = jnp.concatenate(
        [
            pltpu.roll(block[first : first + 8], (width - 8 - first) % BLK, 1)
            for first in range(0, BLK, 8)
        ],
        axis=0,
    )
    left = 7 - lax.broadcasted_iota(jnp.int32, (BLK, BLK), 0) % 8
    for shift in (1, 2, 4):
        turned = jnp.where(left & shift != 0, pltpu.roll(turned, shift, 1), turned)
    return turned.T[:width, :]


def bands_of(block, width):
    band = take_band(block, width)
    return [band[width - 1 - k : width - k, :] for k in range(width)]


def put_band(band, first):
    padded = jnp.concatenate((band, jnp.zeros((BLK - BAND, BLK), F32)), axis=0)
    return pltpu.roll(padded.T, first % BLK, 1, stride=1, stride_axis=0)


def half_angle(gap, twice):
    gap_size = jnp.abs(gap)
    twice_size = jnp.abs(twice)
    largest = jnp.maximum(gap_size, twice_size)
    scale = jnp.where(largest < 2.0**-20, 2.0**80, 1.0)
    gap_size = jnp.where(largest > 0.0, gap_size * scale, 1.0)
    twice_size = twice_size * scale
    inverse = lax.rsqrt(gap_size * gap_size + twice_size * twice_size)
    half = 0.5 + (0.5 * gap_size) * inverse
    half_inverse = lax.rsqrt(half)
    large = half * half_inverse
    small = (0.5 * twice_size) * inverse * half_inverse
    sign = jnp.where(twice < 0.0, -1.0, 1.0)
    ahead = gap >= 0.0
    return jnp.where(ahead, large, small), sign * jnp.where(ahead, small, large)


def row_copies(rows, index):
    return jnp.broadcast_to(rows[index : index + 1, :], (8, BLK))


def ahead_by_one(rows):
    return pltpu.roll(rows, 1, 1)


def jacobi_bands(uu, ul, lu, ll):
    last = BAND - 1
    is_first = lax.broadcasted_iota(jnp.int32, (BAND, BLK), 0) == 0
    row_ids = lax.broadcasted_iota(jnp.int32, (BAND, BLK), 0)
    one = jnp.where(row_ids == last, 1.0, 0.0).astype(F32)
    zero = jnp.zeros((BAND, BLK), F32)
    u_top, u_low, l_top, l_low = one, zero, zero, one
    u_diag, l_diag, coupling = row_copies(uu, 0), row_copies(ll, 0), row_copies(ul, 0)
    for step in range(STEPS):
        cos, sin = half_angle(u_diag - l_diag, 2.0 * coupling)
        final_step = step == STEPS - 1
        if not final_step:
            u_past, l_past, x_past = (ahead_by_one(v) for v in (u_diag, l_diag, coupling))
            cos_past, sin_past = ahead_by_one(cos), ahead_by_one(sin)
            u_diag, coupling = (
                cos * (cos * u_diag + sin * coupling) + sin * (cos * coupling + sin * l_diag),
                cos_past * (cos * row_copies(ul, 1) + sin * row_copies(ll, 1))
                - sin_past * (cos * row_copies(uu, 1) + sin * row_copies(lu, 1)),
            )
            l_diag = cos_past * (cos_past * l_past - sin_past * x_past) - sin_past * (
                cos_past * x_past - sin_past * u_past
            )
        cos_b = jnp.concatenate([cos] * (BAND // 8), axis=0)
        sin_b = jnp.concatenate([sin] * (BAND // 8), axis=0)
        u_top, l_top = u_top * cos_b + l_top * sin_b, l_top * cos_b - u_top * sin_b
        u_low, l_low = u_low * cos_b + l_low * sin_b, l_low * cos_b - u_low * sin_b
        if final_step:
            break
        cos_d = jnp.concatenate(
            [pltpu.roll(cos, 8 * i, 1, stride=1, stride_axis=0) for i in range(BAND // 8)], axis=0
        )
        sin_d = jnp.concatenate(
            [pltpu.roll(sin, 8 * i, 1, stride=1, stride_axis=0) for i in range(BAND // 8)], axis=0
        )
        uu, lu = uu * cos_b + lu * sin_b, lu * cos_b - uu * sin_b
        ul, ll = ul * cos_b + ll * sin_b, ll * cos_b - ul * sin_b
        uu, ul = uu * cos_d + ul * sin_d, ul * cos_d - uu * sin_d
        lu, ll = lu * cos_d + ll * sin_d, ll * cos_d - lu * sin_d
        ul = pltpu.roll(ul, last, 0)
        lu = jnp.where(is_first, ul, ahead_by_one(pltpu.roll(lu, 1, 0)))
        ll = ahead_by_one(ll)
        l_top = ahead_by_one(pltpu.roll(l_top, last, 0))
        l_low = ahead_by_one(pltpu.roll(l_low, last, 0))
    back = BLK - last
    l_top, l_low = pltpu.roll(l_top, back, 1), pltpu.roll(l_low, back, 1)
    return u_top, u_low, l_top, l_low


def turned_half(top, low, first):
    return jnp.concatenate((put_band(top, first), put_band(low, first)), axis=1)


def times_turned(tile, turned):
    high, low = split(tile)
    turned_high, turned_low = split(turned)
    last = ((1,), (1,))
    return mm(high, turned_high, last) + (mm(high, turned_low, last) + mm(low, turned_high, last))


def all_bands(gram):
    rows = []
    for top in (0, BLK):
        for left in (0, BLK):
            rows += bands_of(gram[top : top + BLK, left : left + BLK], BAND)
    return jnp.concatenate(rows, axis=0)


def summed(parts_ref):
    total = parts_ref[0]
    for i in range(1, parts_ref.shape[0]):
        total = total + parts_ref[i]
    return total


def blocks(bands):
    return [bands[BAND * i : BAND * (i + 1)] for i in range(4)]


VMEM_SPEC = pl.BlockSpec(memory_space=pltpu.VMEM)
PARAMS = pltpu.CompilerParams(vmem_limit_bytes=LIMIT)


def early_kernel(cols_ref, early_ref, sems):
    step = EARLY // sems.shape[0]
    copies = [
        pltpu.make_async_copy(
            cols_ref.at[pl.ds(i * step, step)], early_ref.at[pl.ds(i * step, step)], sems.at[i]
        )
        for i in range(sems.shape[0])
    ]
    for copy in copies:
        copy.start()
    for copy in copies:
        copy.wait()


def early_rows(cols):
    return pl.pallas_call(
        early_kernel,
        in_specs=[pl.BlockSpec(memory_space=pltpu.HBM)],
        out_specs=VMEM_SPEC,
        out_shape=pltpu.VMEM((EARLY, 2 * BLK), F32),
        scratch_shapes=[pltpu.SemaphoreType.DMA((4,))],
        name="early_rows",
    )(cols)


def gram_kernel(cols_ref, bands_ref):
    bands_ref[...] = all_bands(gram_tile(cols_ref[...]))


def gram_bands(cols):
    return pl.pallas_call(
        gram_kernel,
        in_specs=[VMEM_SPEC],
        out_shape=jax.ShapeDtypeStruct((ROWS, BLK), F32),
        compiler_params=PARAMS,
        name="gram_bands",
    )(cols)


def jacobi_kernel(parts_ref, cols_ref, own_ref, late_ref, trace_ref):
    bands = summed(parts_ref)
    uu, ul, lu, ll = blocks(bands)
    trace_ref[...] = jnp.broadcast_to((uu[:1] + ll[:1])[None], trace_ref.shape)
    u_top, u_low, l_top, l_low = jacobi_bands(uu, ul, lu, ll)
    own_ref[...] = jnp.concatenate((u_top, u_low), axis=0)
    late_ref[: 2 * BAND, :] = jnp.concatenate((l_top, l_low), axis=0)
    late_ref[2 * BAND :, :] = times_turned(cols_ref[EARLY:, :], turned_half(l_top, l_low, 0))


def jacobi(parts, cols, copies):
    return pl.pallas_call(
        jacobi_kernel,
        in_specs=[VMEM_SPEC, VMEM_SPEC],
        out_shape=(
            pltpu.VMEM((2 * BAND, BLK), F32),
            jax.ShapeDtypeStruct((2 * BAND + cols.shape[0] - EARLY, BLK), F32),
            jax.ShapeDtypeStruct((copies, 1, BLK), F32),
        ),
        compiler_params=PARAMS,
        name="jacobi",
    )(parts, cols)


def upper_kernel(cols_ref, own_ref, upper_ref, bands_ref):
    upper = times_turned(cols_ref[...], turned_half(own_ref[:BAND, :], own_ref[BAND:, :], 1 - BAND))
    upper_ref[...] = upper
    high, low = split(upper)
    rows = ((0,), (0,))
    cross = mm(high, low, rows)
    gram = mm(high, high, rows) + mm(low, low, rows) + (cross + cross.T)
    bands_ref[...] = jnp.concatenate(bands_of(gram, BAND), axis=0)


def upper_half(cols, own):
    return pl.pallas_call(
        upper_kernel,
        in_specs=[VMEM_SPEC, VMEM_SPEC],
        out_shape=(
            jax.ShapeDtypeStruct((cols.shape[0], BLK), F32),
            jax.ShapeDtypeStruct((BAND, BLK), F32),
        ),
        cost_estimate=COST,
        compiler_params=PARAMS,
        name="upper_half",
    )(cols, own)


def lower_gram(upper, lower):
    low_high, low_low = split(lower)
    pair_high, pair_low = split(jnp.concatenate((upper, lower), axis=1))
    rows = ((0,), (0,))
    return (
        mm(low_high, pair_high, rows)
        + mm(low_low, pair_low, rows)
        + (mm(low_high, pair_low, rows) + mm(low_low, pair_high, rows))
    )


def link_kernel(raw_ref, late_ref, upper_ref, uu_ref, pair_ref, bands_ref, turned_ref, total_ref):
    step = pl.program_id(0)

    @pl.when(step == 0)
    def _():
        turned_ref[...] = turned_half(late_ref[:BAND, :], late_ref[BAND : 2 * BAND, :], 0)
        late = late_ref[2 * BAND :, :]
        upper = upper_ref[EARLY:, :]
        pair_ref[EARLY:, :BLK] = upper
        pair_ref[EARLY:, BLK:] = late
        total_ref[...] = lower_gram(upper, late)

    tile = raw_ref.shape[0]
    rows = pl.ds(pl.multiple_of(step * tile, 8), tile)
    lower = times_turned(raw_ref[...], turned_ref[...])
    upper = upper_ref[rows, :]
    pair_ref[rows, :BLK] = upper
    pair_ref[rows, BLK:] = lower
    total_ref[...] += lower_gram(upper, lower)

    @pl.when(step == pl.num_programs(0) - 1)
    def _():
        total = total_ref[...]
        lu, ll = total[:, :BLK], total[:, BLK:]
        bands_ref[:BAND, :] = uu_ref[...]
        bands_ref[BAND:, :] = jnp.concatenate(
            bands_of(lu.T, BAND) + bands_of(lu, BAND) + bands_of(ll, BAND), axis=0
        )


def link(raw, late, upper, uu):
    rows = upper.shape[0]
    return pl.pallas_call(
        link_kernel,
        grid=(2,),
        in_specs=[
            pl.BlockSpec((EARLY // 2, 2 * BLK), lambda i: (i, 0)),
            pl.BlockSpec(late.shape, lambda i: (0, 0)),
            pl.BlockSpec(upper.shape, lambda i: (0, 0)),
            pl.BlockSpec(uu.shape, lambda i: (0, 0)),
        ],
        out_specs=(
            pl.BlockSpec((rows, 2 * BLK), lambda i: (0, 0)),
            pl.BlockSpec((ROWS, BLK), lambda i: (0, 0)),
        ),
        out_shape=(
            jax.ShapeDtypeStruct((rows, 2 * BLK), F32),
            jax.ShapeDtypeStruct((ROWS, BLK), F32),
        ),
        scratch_shapes=[pltpu.VMEM((BLK, 2 * BLK), F32), pltpu.VMEM((BLK, 2 * BLK), F32)],
        cost_estimate=COST,
        compiler_params=PARAMS,
        name="link",
    )(raw, late, upper, uu)


def final_kernel(
    entry_count, parts_ref, traces_ref, pair_ref, out_ref, tiles_ref, high_ref, low_ref, sems
):
    rms = jnp.sqrt(jnp.sum(summed(traces_ref), axis=1, keepdims=True) / entry_count)
    u_top, u_low, l_top, l_low = jacobi_bands(*blocks(summed(parts_ref)))
    for first, turned in (
        (0, turned_half(u_top, u_low, 1 - BAND)),
        (BLK, turned_half(l_top, l_low, 0)),
    ):
        high, low = split(turned / rms)
        high_ref[first : first + BLK, :] = high
        low_ref[first : first + BLK, :] = low
    last = ((1,), (1,))
    stores = []
    for i in range(tiles_ref.shape[0]):
        rows = pl.ds(i * PART, PART)
        high, low = split(pair_ref[rows, :])
        tiles_ref[i] = mm(high, high_ref[...], last) + (
            mm(high, low_ref[...], last) + mm(low, high_ref[...], last)
        )
        store = pltpu.make_async_copy(tiles_ref.at[i], out_ref.at[rows], sems.at[i])
        store.start()
        stores.append(store)
    for store in stores:
        store.wait()


def final(entry_count, parts, traces, pair):
    rows = pair.shape[0]
    count = rows // PART
    return pl.pallas_call(
        functools.partial(final_kernel, entry_count),
        in_specs=[VMEM_SPEC] * 3,
        out_specs=pl.BlockSpec(memory_space=pltpu.HBM),
        out_shape=jax.ShapeDtypeStruct((rows, 2 * BLK), F32),
        scratch_shapes=[
            pltpu.VMEM((count, PART, 2 * BLK), F32),
            pltpu.VMEM((2 * BLK, 2 * BLK), BF16),
            pltpu.VMEM((2 * BLK, 2 * BLK), BF16),
            pltpu.SemaphoreType.DMA((count,)),
        ],
        compiler_params=PARAMS,
        name="final",
    )(parts, traces, pair)


def to_next(value):
    count = lax.axis_size("pair")
    return lax.ppermute(value, "pair", [(pair, (pair + 1) % count) for pair in range(count)])


def body(activations):
    pairs, rows = lax.axis_size("pair"), lax.axis_size("row")
    entry_count = activations.shape[0] * activations.shape[1] * pairs * rows

    raw = to_next(early_rows(activations))
    bands = gram_bands(activations)
    own, late, traces = jacobi(lax.all_gather(bands, "row"), activations, pairs)
    late = to_next(late)
    traces = lax.all_to_all(traces, "pair", 0, 0, tiled=True)
    upper, uu = upper_half(activations, own)
    pair, bands = link(raw, late, upper, uu)
    bands, traces = lax.optimization_barrier((bands, traces))
    parts = lax.all_gather(bands, "row")
    return final(float(entry_count), parts, traces, pair)


def solution(mesh):
    return jax.shard_map(
        body,
        mesh=mesh,
        in_specs=(P("row", "pair"),),
        out_specs=P("row", "pair"),
        check_vma=False,
    )
```

```python
import functools

import jax
import jax.numpy as jnp
from jax import lax
from jax.experimental import pallas as pl
from jax.experimental.pallas import tpu as pltpu
from jax.sharding import PartitionSpec as P

STEPS = 16
BLK = 128
BAND = 16
ROWS = 4 * BAND
TILE = 1024
EARLY = 1088
PART = 256
LIMIT = 24 << 20
COST = pl.CostEstimate(flops=2_000_000_000, bytes_accessed=6_000_000, transcendentals=0)
F32 = jnp.float32
BF16 = jnp.bfloat16


def split(value):
    high = value.astype(BF16)
    return high, (value - high.astype(F32)).astype(BF16)


def mm(left, right, dims):
    return lax.dot_general(left, right, (dims, ((), ())), preferred_element_type=F32)


def gram_tile(tile):
    high, low = split(tile)
    rows = ((0,), (0,))
    cross = mm(high, low, rows)
    return mm(high, high, rows) + mm(low, low, rows) + (cross + cross.T)


def take_band(block, width):
    turned = jnp.concatenate(
        [
            pltpu.roll(block[first : first + 8], (width - 8 - first) % BLK, 1)
            for first in range(0, BLK, 8)
        ],
        axis=0,
    )
    left = 7 - lax.broadcasted_iota(jnp.int32, (BLK, BLK), 0) % 8
    for shift in (1, 2, 4):
        turned = jnp.where(left & shift != 0, pltpu.roll(turned, shift, 1), turned)
    return turned.T[:width, :]


def bands_of(block, width):
    band = take_band(block, width)
    return [band[width - 1 - k : width - k, :] for k in range(width)]


def put_band(band, first):
    padded = jnp.concatenate((band, jnp.zeros((BLK - BAND, BLK), F32)), axis=0)
    return pltpu.roll(padded.T, first % BLK, 1, stride=1, stride_axis=0)


def half_angle(gap, twice):
    gap_size = jnp.abs(gap)
    twice_size = jnp.abs(twice)
    largest = jnp.maximum(gap_size, twice_size)
    scale = jnp.where(largest < 2.0**-20, 2.0**80, 1.0)
    gap_size = jnp.where(largest > 0.0, gap_size * scale, 1.0)
    twice_size = twice_size * scale
    inverse = lax.rsqrt(gap_size * gap_size + twice_size * twice_size)
    half = 0.5 + (0.5 * gap_size) * inverse
    half_inverse = lax.rsqrt(half)
    large = half * half_inverse
    small = (0.5 * twice_size) * inverse * half_inverse
    sign = jnp.where(twice < 0.0, -1.0, 1.0)
    ahead = gap >= 0.0
    return jnp.where(ahead, large, small), sign * jnp.where(ahead, small, large)


def row_copies(rows, index):
    return jnp.broadcast_to(rows[index : index + 1, :], (8, BLK))


def ahead_by_one(rows):
    return pltpu.roll(rows, 1, 1)


def jacobi_bands(uu, ul, lu, ll):
    last = BAND - 1
    is_first = lax.broadcasted_iota(jnp.int32, (BAND, BLK), 0) == 0
    row_ids = lax.broadcasted_iota(jnp.int32, (BAND, BLK), 0)
    one = jnp.where(row_ids == last, 1.0, 0.0).astype(F32)
    zero = jnp.zeros((BAND, BLK), F32)
    u_top, u_low, l_top, l_low = one, zero, zero, one
    u_diag, l_diag, coupling = row_copies(uu, 0), row_copies(ll, 0), row_copies(ul, 0)
    for step in range(STEPS):
        cos, sin = half_angle(u_diag - l_diag, 2.0 * coupling)
        final_step = step == STEPS - 1
        if not final_step:
            u_past, l_past, x_past = (ahead_by_one(v) for v in (u_diag, l_diag, coupling))
            cos_past, sin_past = ahead_by_one(cos), ahead_by_one(sin)
            u_diag, coupling = (
                cos * (cos * u_diag + sin * coupling) + sin * (cos * coupling + sin * l_diag),
                cos_past * (cos * row_copies(ul, 1) + sin * row_copies(ll, 1))
                - sin_past * (cos * row_copies(uu, 1) + sin * row_copies(lu, 1)),
            )
            l_diag = cos_past * (cos_past * l_past - sin_past * x_past) - sin_past * (
                cos_past * x_past - sin_past * u_past
            )
        cos_b = jnp.concatenate([cos] * (BAND // 8), axis=0)
        sin_b = jnp.concatenate([sin] * (BAND // 8), axis=0)
        u_top, l_top = u_top * cos_b + l_top * sin_b, l_top * cos_b - u_top * sin_b
        u_low, l_low = u_low * cos_b + l_low * sin_b, l_low * cos_b - u_low * sin_b
        if final_step:
            break
        cos_d = jnp.concatenate(
            [pltpu.roll(cos, 8 * i, 1, stride=1, stride_axis=0) for i in range(BAND // 8)], axis=0
        )
        sin_d = jnp.concatenate(
            [pltpu.roll(sin, 8 * i, 1, stride=1, stride_axis=0) for i in range(BAND // 8)], axis=0
        )
        uu, lu = uu * cos_b + lu * sin_b, lu * cos_b - uu * sin_b
        ul, ll = ul * cos_b + ll * sin_b, ll * cos_b - ul * sin_b
        uu, ul = uu * cos_d + ul * sin_d, ul * cos_d - uu * sin_d
        lu, ll = lu * cos_d + ll * sin_d, ll * cos_d - lu * sin_d
        ul = pltpu.roll(ul, last, 0)
        lu = jnp.where(is_first, ul, ahead_by_one(pltpu.roll(lu, 1, 0)))
        ll = ahead_by_one(ll)
        l_top = ahead_by_one(pltpu.roll(l_top, last, 0))
        l_low = ahead_by_one(pltpu.roll(l_low, last, 0))
    back = BLK - last
    l_top, l_low = pltpu.roll(l_top, back, 1), pltpu.roll(l_low, back, 1)
    return u_top, u_low, l_top, l_low


def turned_half(top, low, first):
    return jnp.concatenate((put_band(top, first), put_band(low, first)), axis=1)


def times_turned(tile, turned):
    high, low = split(tile)
    turned_high, turned_low = split(turned)
    last = ((1,), (1,))
    return mm(high, turned_high, last) + (mm(high, turned_low, last) + mm(low, turned_high, last))


def all_bands(gram):
    rows = []
    for top in (0, BLK):
        for left in (0, BLK):
            rows += bands_of(gram[top : top + BLK, left : left + BLK], BAND)
    return jnp.concatenate(rows, axis=0)


def summed(parts_ref):
    total = parts_ref[0]
    for i in range(1, parts_ref.shape[0]):
        total = total + parts_ref[i]
    return total


def blocks(bands):
    return [bands[BAND * i : BAND * (i + 1)] for i in range(4)]


VMEM_SPEC = pl.BlockSpec(memory_space=pltpu.VMEM)
PARAMS = pltpu.CompilerParams(vmem_limit_bytes=LIMIT)


def early_kernel(cols_ref, early_ref, sems):
    step = EARLY // sems.shape[0]
    copies = [
        pltpu.make_async_copy(
            cols_ref.at[pl.ds(i * step, step)], early_ref.at[pl.ds(i * step, step)], sems.at[i]
        )
        for i in range(sems.shape[0])
    ]
    for copy in copies:
        copy.start()
    for copy in copies:
        copy.wait()


def early_rows(cols):
    return pl.pallas_call(
        early_kernel,
        in_specs=[pl.BlockSpec(memory_space=pltpu.HBM)],
        out_specs=VMEM_SPEC,
        out_shape=pltpu.VMEM((EARLY, 2 * BLK), F32),
        scratch_shapes=[pltpu.SemaphoreType.DMA((4,))],
        name="early_rows",
    )(cols)


def gram_kernel(cols_ref, bands_ref):
    bands_ref[...] = all_bands(gram_tile(cols_ref[...]))


def gram_bands(cols):
    return pl.pallas_call(
        gram_kernel,
        in_specs=[VMEM_SPEC],
        out_shape=jax.ShapeDtypeStruct((ROWS, BLK), F32),
        compiler_params=PARAMS,
        name="gram_bands",
    )(cols)


def jacobi_kernel(parts_ref, cols_ref, own_ref, late_ref, trace_ref):
    bands = summed(parts_ref)
    uu, ul, lu, ll = blocks(bands)
    trace_ref[...] = jnp.broadcast_to((uu[:1] + ll[:1])[None], trace_ref.shape)
    u_top, u_low, l_top, l_low = jacobi_bands(uu, ul, lu, ll)
    own_ref[...] = jnp.concatenate((u_top, u_low), axis=0)
    late_ref[: 2 * BAND, :] = jnp.concatenate((l_top, l_low), axis=0)
    late_ref[2 * BAND :, :] = times_turned(cols_ref[EARLY:, :], turned_half(l_top, l_low, 0))


def jacobi(parts, cols, copies):
    return pl.pallas_call(
        jacobi_kernel,
        in_specs=[VMEM_SPEC, VMEM_SPEC],
        out_shape=(
            pltpu.VMEM((2 * BAND, BLK), F32),
            jax.ShapeDtypeStruct((2 * BAND + cols.shape[0] - EARLY, BLK), F32),
            jax.ShapeDtypeStruct((copies, 1, BLK), F32),
        ),
        compiler_params=PARAMS,
        name="jacobi",
    )(parts, cols)


def halves_times_turned(high, low, turned):
    turned_high, turned_low = split(turned)
    last = ((1,), (1,))
    return mm(high, turned_high, last) + (mm(high, turned_low, last) + mm(low, turned_high, last))


def upper_kernel(
    cols_ref, own_ref, raw_ref, upper_high, upper_low, raw_high, raw_low, bands_ref, raw_tiles, sems
):
    count = sems.shape[0]
    step = EARLY // count
    loads = [
        pltpu.make_async_copy(raw_ref.at[pl.ds(i * step, step)], raw_tiles.at[pl.ds(i * step, step)], sems.at[i])
        for i in range(count)
    ]
    for load in loads:
        load.start()
    upper = times_turned(cols_ref[...], turned_half(own_ref[:BAND, :], own_ref[BAND:, :], 1 - BAND))
    high, low = split(upper)
    upper_high[...] = high
    upper_low[...] = low
    rows = ((0,), (0,))
    cross = mm(high, low, rows)
    gram = mm(high, high, rows) + mm(low, low, rows) + (cross + cross.T)
    bands_ref[...] = jnp.concatenate(bands_of(gram, BAND), axis=0)
    for load in loads:
        load.wait()
    high, low = split(raw_tiles[...])
    raw_high[...] = high
    raw_low[...] = low


def upper_half(cols, own, raw):
    rows = cols.shape[0]
    upper = jax.ShapeDtypeStruct((rows, BLK), BF16)
    early = jax.ShapeDtypeStruct(raw.shape, BF16)
    return pl.pallas_call(
        upper_kernel,
        in_specs=[VMEM_SPEC, VMEM_SPEC, pl.BlockSpec(memory_space=pltpu.HBM)],
        out_shape=(upper, upper, early, early, jax.ShapeDtypeStruct((BAND, BLK), F32)),
        scratch_shapes=[pltpu.VMEM(raw.shape, F32), pltpu.SemaphoreType.DMA((2,))],
        cost_estimate=COST,
        compiler_params=PARAMS,
        name="upper_half",
    )(cols, own, raw)


def link_kernel(raw_high, raw_low, late_ref, upper_high, upper_low, uu_ref, pair_high, pair_low, bands_ref):
    turned = turned_half(late_ref[:BAND, :], late_ref[BAND : 2 * BAND, :], 0)
    early_high, early_low = split(halves_times_turned(raw_high[...], raw_low[...], turned))
    late_high, late_low = split(late_ref[2 * BAND :, :])
    pair_high[:, :BLK] = upper_high[...]
    pair_low[:, :BLK] = upper_low[...]
    pair_high[:EARLY, BLK:] = early_high
    pair_low[:EARLY, BLK:] = early_low
    pair_high[EARLY:, BLK:] = late_high
    pair_low[EARLY:, BLK:] = late_low
    high, low = pair_high[...], pair_low[...]
    lower_high, lower_low = high[:, BLK:], low[:, BLK:]
    rows = ((0,), (0,))
    gram = (
        mm(lower_high, high, rows)
        + mm(lower_low, low, rows)
        + (mm(lower_high, low, rows) + mm(lower_low, high, rows))
    )
    lu, ll = gram[:, :BLK], gram[:, BLK:]
    bands_ref[:BAND, :] = uu_ref[...]
    bands_ref[BAND:, :] = jnp.concatenate(
        bands_of(lu.T, BAND) + bands_of(lu, BAND) + bands_of(ll, BAND), axis=0
    )


def link(early, late, upper, uu):
    rows = upper[0].shape[0]
    pair = jax.ShapeDtypeStruct((rows, 2 * BLK), BF16)
    return pl.pallas_call(
        link_kernel,
        in_specs=[VMEM_SPEC] * 6,
        out_shape=(pair, pair, jax.ShapeDtypeStruct((ROWS, BLK), F32)),
        cost_estimate=COST,
        compiler_params=PARAMS,
        name="link",
    )(*early, late, *upper, uu)


def final_kernel(
    entry_count, parts_ref, traces_ref, pair_high, pair_low, out_ref, tiles_ref, high_ref, low_ref, sems
):
    rms = jnp.sqrt(jnp.sum(summed(traces_ref), axis=1, keepdims=True) / entry_count)
    u_top, u_low, l_top, l_low = jacobi_bands(*blocks(summed(parts_ref)))
    for first, turned in (
        (0, turned_half(u_top, u_low, 1 - BAND)),
        (BLK, turned_half(l_top, l_low, 0)),
    ):
        high, low = split(turned / rms)
        high_ref[first : first + BLK, :] = high
        low_ref[first : first + BLK, :] = low
    last = ((1,), (1,))
    stores = []
    for i in range(tiles_ref.shape[0]):
        rows = pl.ds(i * PART, PART)
        high, low = pair_high[rows, :], pair_low[rows, :]
        tiles_ref[i] = mm(high, high_ref[...], last) + (
            mm(high, low_ref[...], last) + mm(low, high_ref[...], last)
        )
        store = pltpu.make_async_copy(tiles_ref.at[i], out_ref.at[rows], sems.at[i])
        store.start()
        stores.append(store)
    for store in stores:
        store.wait()


def final(entry_count, parts, traces, pair):
    rows = pair[0].shape[0]
    count = rows // PART
    return pl.pallas_call(
        functools.partial(final_kernel, entry_count),
        in_specs=[VMEM_SPEC] * 4,
        out_specs=pl.BlockSpec(memory_space=pltpu.HBM),
        out_shape=jax.ShapeDtypeStruct((rows, 2 * BLK), F32),
        scratch_shapes=[
            pltpu.VMEM((count, PART, 2 * BLK), F32),
            pltpu.VMEM((2 * BLK, 2 * BLK), BF16),
            pltpu.VMEM((2 * BLK, 2 * BLK), BF16),
            pltpu.SemaphoreType.DMA((count,)),
        ],
        compiler_params=PARAMS,
        name="final",
    )(parts, traces, *pair)


def to_next(value):
    count = lax.axis_size("pair")
    return lax.ppermute(value, "pair", [(pair, (pair + 1) % count) for pair in range(count)])


def body(activations):
    pairs, rows = lax.axis_size("pair"), lax.axis_size("row")
    entry_count = activations.shape[0] * activations.shape[1] * pairs * rows

    raw = to_next(early_rows(activations))
    bands = gram_bands(activations)
    own, late, traces = jacobi(lax.all_gather(bands, "row"), activations, pairs)
    late = to_next(late)
    traces = lax.all_to_all(traces, "pair", 0, 0, tiled=True)
    upper_high, upper_low, early_high, early_low, uu = upper_half(activations, own, raw)
    *pair, bands = link((early_high, early_low), late, (upper_high, upper_low), uu)
    bands, traces = lax.optimization_barrier((bands, traces))
    parts = lax.all_gather(bands, "row")
    return final(float(entry_count), parts, traces, pair)


def solution(mesh):
    return jax.shard_map(
        body,
        mesh=mesh,
        in_specs=(P("row", "pair"),),
        out_specs=P("row", "pair"),
        check_vma=False,
    )
```

```python
import functools

import jax
import jax.numpy as jnp
from jax import lax
from jax.experimental import pallas as pl
from jax.experimental.pallas import tpu as pltpu
from jax.sharding import PartitionSpec as P

STEPS = 16
BLK = 128
BAND = 16
ROWS = 4 * BAND
TILE = 1024
EARLY = 1088
PART = 256
LIMIT = 24 << 20
COST = pl.CostEstimate(flops=2_000_000_000, bytes_accessed=6_000_000, transcendentals=0)
F32 = jnp.float32
BF16 = jnp.bfloat16


def split(value):
    high = value.astype(BF16)
    return high, (value - high.astype(F32)).astype(BF16)


def mm(left, right, dims):
    return lax.dot_general(left, right, (dims, ((), ())), preferred_element_type=F32)


def gram_tile(tile):
    high, low = split(tile)
    rows = ((0,), (0,))
    cross = mm(high, low, rows)
    return mm(high, high, rows) + mm(low, low, rows) + (cross + cross.T)


def take_band(block, width):
    turned = jnp.concatenate(
        [
            pltpu.roll(block[first : first + 8], (width - 8 - first) % BLK, 1)
            for first in range(0, BLK, 8)
        ],
        axis=0,
    )
    left = 7 - lax.broadcasted_iota(jnp.int32, (BLK, BLK), 0) % 8
    for shift in (1, 2, 4):
        turned = jnp.where(left & shift != 0, pltpu.roll(turned, shift, 1), turned)
    return turned.T[:width, :]


def bands_of(block, width):
    band = take_band(block, width)
    return [band[width - 1 - k : width - k, :] for k in range(width)]


def put_band(band, first):
    padded = jnp.concatenate((band, jnp.zeros((BLK - BAND, BLK), F32)), axis=0)
    return pltpu.roll(padded.T, first % BLK, 1, stride=1, stride_axis=0)


def half_angle(gap, twice):
    gap_size = jnp.abs(gap)
    twice_size = jnp.abs(twice)
    largest = jnp.maximum(gap_size, twice_size)
    scale = jnp.where(largest < 2.0**-20, 2.0**80, 1.0)
    gap_size = jnp.where(largest > 0.0, gap_size * scale, 1.0)
    twice_size = twice_size * scale
    inverse = lax.rsqrt(gap_size * gap_size + twice_size * twice_size)
    half = 0.5 + (0.5 * gap_size) * inverse
    half_inverse = lax.rsqrt(half)
    large = half * half_inverse
    small = (0.5 * twice_size) * inverse * half_inverse
    sign = jnp.where(twice < 0.0, -1.0, 1.0)
    ahead = gap >= 0.0
    return jnp.where(ahead, large, small), sign * jnp.where(ahead, small, large)


def row_copies(rows, index):
    return jnp.broadcast_to(rows[index : index + 1, :], (8, BLK))


def ahead_by_one(rows):
    return pltpu.roll(rows, 1, 1)


def jacobi_bands(uu, ul, lu, ll):
    last = BAND - 1
    is_first = lax.broadcasted_iota(jnp.int32, (BAND, BLK), 0) == 0
    row_ids = lax.broadcasted_iota(jnp.int32, (BAND, BLK), 0)
    one = jnp.where(row_ids == last, 1.0, 0.0).astype(F32)
    zero = jnp.zeros((BAND, BLK), F32)
    u_top, u_low, l_top, l_low = one, zero, zero, one
    u_diag, l_diag, coupling = row_copies(uu, 0), row_copies(ll, 0), row_copies(ul, 0)
    for step in range(STEPS):
        cos, sin = half_angle(u_diag - l_diag, 2.0 * coupling)
        final_step = step == STEPS - 1
        if not final_step:
            u_past, l_past, x_past = (ahead_by_one(v) for v in (u_diag, l_diag, coupling))
            cos_past, sin_past = ahead_by_one(cos), ahead_by_one(sin)
            u_diag, coupling = (
                cos * (cos * u_diag + sin * coupling) + sin * (cos * coupling + sin * l_diag),
                cos_past * (cos * row_copies(ul, 1) + sin * row_copies(ll, 1))
                - sin_past * (cos * row_copies(uu, 1) + sin * row_copies(lu, 1)),
            )
            l_diag = cos_past * (cos_past * l_past - sin_past * x_past) - sin_past * (
                cos_past * x_past - sin_past * u_past
            )
        cos_b = jnp.concatenate([cos] * (BAND // 8), axis=0)
        sin_b = jnp.concatenate([sin] * (BAND // 8), axis=0)
        u_top, l_top = u_top * cos_b + l_top * sin_b, l_top * cos_b - u_top * sin_b
        u_low, l_low = u_low * cos_b + l_low * sin_b, l_low * cos_b - u_low * sin_b
        if final_step:
            break
        cos_d = jnp.concatenate(
            [pltpu.roll(cos, 8 * i, 1, stride=1, stride_axis=0) for i in range(BAND // 8)], axis=0
        )
        sin_d = jnp.concatenate(
            [pltpu.roll(sin, 8 * i, 1, stride=1, stride_axis=0) for i in range(BAND // 8)], axis=0
        )
        uu, lu = uu * cos_b + lu * sin_b, lu * cos_b - uu * sin_b
        ul, ll = ul * cos_b + ll * sin_b, ll * cos_b - ul * sin_b
        uu, ul = uu * cos_d + ul * sin_d, ul * cos_d - uu * sin_d
        lu, ll = lu * cos_d + ll * sin_d, ll * cos_d - lu * sin_d
        ul = pltpu.roll(ul, last, 0)
        lu = jnp.where(is_first, ul, ahead_by_one(pltpu.roll(lu, 1, 0)))
        ll = ahead_by_one(ll)
        l_top = ahead_by_one(pltpu.roll(l_top, last, 0))
        l_low = ahead_by_one(pltpu.roll(l_low, last, 0))
    back = BLK - last
    l_top, l_low = pltpu.roll(l_top, back, 1), pltpu.roll(l_low, back, 1)
    return u_top, u_low, l_top, l_low


def turned_half(top, low, first):
    return jnp.concatenate((put_band(top, first), put_band(low, first)), axis=1)


def times_turned(tile, turned):
    high, low = split(tile)
    turned_high, turned_low = split(turned)
    last = ((1,), (1,))
    return mm(high, turned_high, last) + (mm(high, turned_low, last) + mm(low, turned_high, last))


def all_bands(gram):
    rows = []
    for top in (0, BLK):
        for left in (0, BLK):
            rows += bands_of(gram[top : top + BLK, left : left + BLK], BAND)
    return jnp.concatenate(rows, axis=0)


def summed(parts_ref):
    total = parts_ref[0]
    for i in range(1, parts_ref.shape[0]):
        total = total + parts_ref[i]
    return total


def blocks(bands):
    return [bands[BAND * i : BAND * (i + 1)] for i in range(4)]


VMEM_SPEC = pl.BlockSpec(memory_space=pltpu.VMEM)
PARAMS = pltpu.CompilerParams(vmem_limit_bytes=LIMIT)


def early_kernel(cols_ref, early_ref, sems):
    step = EARLY // sems.shape[0]
    copies = [
        pltpu.make_async_copy(
            cols_ref.at[pl.ds(i * step, step)], early_ref.at[pl.ds(i * step, step)], sems.at[i]
        )
        for i in range(sems.shape[0])
    ]
    for copy in copies:
        copy.start()
    for copy in copies:
        copy.wait()


def early_rows(cols):
    return pl.pallas_call(
        early_kernel,
        in_specs=[pl.BlockSpec(memory_space=pltpu.HBM)],
        out_specs=VMEM_SPEC,
        out_shape=pltpu.VMEM((EARLY, 2 * BLK), F32),
        scratch_shapes=[pltpu.SemaphoreType.DMA((4,))],
        name="early_rows",
    )(cols)


def gram_kernel(cols_ref, bands_ref):
    bands_ref[...] = all_bands(gram_tile(cols_ref[...]))


def gram_bands(cols):
    return pl.pallas_call(
        gram_kernel,
        in_specs=[VMEM_SPEC],
        out_shape=jax.ShapeDtypeStruct((ROWS, BLK), F32),
        compiler_params=PARAMS,
        name="gram_bands",
    )(cols)


def jacobi_kernel(parts_ref, cols_ref, own_ref, late_ref, trace_ref):
    bands = summed(parts_ref)
    uu, ul, lu, ll = blocks(bands)
    trace_ref[...] = uu[:8] + ll[:8]
    u_top, u_low, l_top, l_low = jacobi_bands(uu, ul, lu, ll)
    own_ref[...] = jnp.concatenate((u_top, u_low), axis=0)
    late_ref[: 2 * BAND, :] = jnp.concatenate((l_top, l_low), axis=0)
    late_ref[2 * BAND :, :] = times_turned(cols_ref[EARLY:, :], turned_half(l_top, l_low, 0))


def jacobi(parts, cols):
    return pl.pallas_call(
        jacobi_kernel,
        in_specs=[VMEM_SPEC, VMEM_SPEC],
        out_shape=(
            pltpu.VMEM((2 * BAND, BLK), F32),
            jax.ShapeDtypeStruct((2 * BAND + cols.shape[0] - EARLY, BLK), F32),
            jax.ShapeDtypeStruct((8, BLK), F32),
        ),
        compiler_params=PARAMS,
        name="jacobi",
    )(parts, cols)


def halves_times_turned(high, low, turned):
    turned_high, turned_low = split(turned)
    last = ((1,), (1,))
    return mm(high, turned_high, last) + (mm(high, turned_low, last) + mm(low, turned_high, last))


def upper_kernel(
    cols_ref, own_ref, raw_ref, upper_high, upper_low, raw_high, raw_low, bands_ref, raw_tiles, sems
):
    count = sems.shape[0]
    step = EARLY // count
    loads = [
        pltpu.make_async_copy(raw_ref.at[pl.ds(i * step, step)], raw_tiles.at[pl.ds(i * step, step)], sems.at[i])
        for i in range(count)
    ]
    for load in loads:
        load.start()
    upper = times_turned(cols_ref[...], turned_half(own_ref[:BAND, :], own_ref[BAND:, :], 1 - BAND))
    high, low = split(upper)
    upper_high[...] = high
    upper_low[...] = low
    rows = ((0,), (0,))
    cross = mm(high, low, rows)
    gram = mm(high, high, rows) + mm(low, low, rows) + (cross + cross.T)
    bands_ref[...] = jnp.concatenate(bands_of(gram, BAND), axis=0)
    for load in loads:
        load.wait()
    high, low = split(raw_tiles[...])
    raw_high[...] = high
    raw_low[...] = low


def upper_half(cols, own, raw):
    rows = cols.shape[0]
    upper = jax.ShapeDtypeStruct((rows, BLK), BF16)
    early = jax.ShapeDtypeStruct(raw.shape, BF16)
    return pl.pallas_call(
        upper_kernel,
        in_specs=[VMEM_SPEC, VMEM_SPEC, pl.BlockSpec(memory_space=pltpu.HBM)],
        out_shape=(upper, upper, early, early, jax.ShapeDtypeStruct((BAND, BLK), F32)),
        scratch_shapes=[pltpu.VMEM(raw.shape, F32), pltpu.SemaphoreType.DMA((2,))],
        cost_estimate=COST,
        compiler_params=PARAMS,
        name="upper_half",
    )(cols, own, raw)


def link_kernel(
    raw_high, raw_low, late_ref, upper_high, upper_low, uu_ref, pair_high, pair_low, bands_ref, late_tiles, sems
):
    loads = []
    for i, (first, size) in enumerate(((0, 2 * BAND), (2 * BAND, late_ref.shape[0] - 2 * BAND))):
        rows = pl.ds(first, size)
        load = pltpu.make_async_copy(late_ref.at[rows], late_tiles.at[rows], sems.at[i])
        load.start()
        loads.append(load)
    pair_high[:, :BLK] = upper_high[...]
    pair_low[:, :BLK] = upper_low[...]
    loads[0].wait()
    turned = turned_half(late_tiles[:BAND, :], late_tiles[BAND : 2 * BAND, :], 0)
    early_high, early_low = split(halves_times_turned(raw_high[...], raw_low[...], turned))
    loads[1].wait()
    late_high, late_low = split(late_tiles[2 * BAND :, :])
    pair_high[:EARLY, BLK:] = early_high
    pair_low[:EARLY, BLK:] = early_low
    pair_high[EARLY:, BLK:] = late_high
    pair_low[EARLY:, BLK:] = late_low
    high, low = pair_high[...], pair_low[...]
    lower_high, lower_low = high[:, BLK:], low[:, BLK:]
    rows = ((0,), (0,))
    gram = (
        mm(lower_high, high, rows)
        + mm(lower_low, low, rows)
        + (mm(lower_high, low, rows) + mm(lower_low, high, rows))
    )
    lu, ll = gram[:, :BLK], gram[:, BLK:]
    bands_ref[:BAND, :] = uu_ref[...]
    bands_ref[BAND:, :] = jnp.concatenate(
        bands_of(lu.T, BAND) + bands_of(lu, BAND) + bands_of(ll, BAND), axis=0
    )


def link(early, late, upper, uu):
    rows = upper[0].shape[0]
    pair = jax.ShapeDtypeStruct((rows, 2 * BLK), BF16)
    return pl.pallas_call(
        link_kernel,
        in_specs=[VMEM_SPEC] * 2 + [pl.BlockSpec(memory_space=pltpu.HBM)] + [VMEM_SPEC] * 3,
        out_shape=(pair, pair, jax.ShapeDtypeStruct((ROWS, BLK), F32)),
        scratch_shapes=[pltpu.VMEM(late.shape, F32), pltpu.SemaphoreType.DMA((2,))],
        cost_estimate=COST,
        compiler_params=PARAMS,
        name="link",
    )(*early, late, *upper, uu)


def final_kernel(
    entry_count, parts_ref, traces_ref, pair_high, pair_low, out_ref, tiles_ref, high_ref, low_ref, sems
):
    rms = jnp.sqrt(jnp.sum(summed(traces_ref), axis=1, keepdims=True) / entry_count)
    u_top, u_low, l_top, l_low = jacobi_bands(*blocks(summed(parts_ref)))
    for first, turned in (
        (0, turned_half(u_top, u_low, 1 - BAND)),
        (BLK, turned_half(l_top, l_low, 0)),
    ):
        high, low = split(turned / rms)
        high_ref[first : first + BLK, :] = high
        low_ref[first : first + BLK, :] = low
    last = ((1,), (1,))
    stores = []
    for i in range(tiles_ref.shape[0]):
        rows = pl.ds(i * PART, PART)
        high, low = pair_high[rows, :], pair_low[rows, :]
        tiles_ref[i] = mm(high, high_ref[...], last) + (
            mm(high, low_ref[...], last) + mm(low, high_ref[...], last)
        )
        store = pltpu.make_async_copy(tiles_ref.at[i], out_ref.at[rows], sems.at[i])
        store.start()
        stores.append(store)
    for store in stores:
        store.wait()


def final(entry_count, parts, traces, pair):
    rows = pair[0].shape[0]
    count = rows // PART
    return pl.pallas_call(
        functools.partial(final_kernel, entry_count),
        in_specs=[VMEM_SPEC] * 4,
        out_specs=pl.BlockSpec(memory_space=pltpu.HBM),
        out_shape=jax.ShapeDtypeStruct((rows, 2 * BLK), F32),
        scratch_shapes=[
            pltpu.VMEM((count, PART, 2 * BLK), F32),
            pltpu.VMEM((2 * BLK, 2 * BLK), BF16),
            pltpu.VMEM((2 * BLK, 2 * BLK), BF16),
            pltpu.SemaphoreType.DMA((count,)),
        ],
        compiler_params=PARAMS,
        name="final",
    )(parts, traces, *pair)


def to_next(value):
    count = lax.axis_size("pair")
    return lax.ppermute(value, "pair", [(pair, (pair + 1) % count) for pair in range(count)])


def body(activations):
    pairs, rows = lax.axis_size("pair"), lax.axis_size("row")
    entry_count = activations.shape[0] * activations.shape[1] * pairs * rows

    raw = to_next(early_rows(activations))
    bands = gram_bands(activations)
    own, late, trace = jacobi(lax.all_gather(bands, "row"), activations)
    late = to_next(late)
    traces = jnp.broadcast_to(trace[:1][None], (pairs, 1, BLK))
    traces = lax.all_to_all(traces, "pair", 0, 0, tiled=True)
    upper_high, upper_low, early_high, early_low, uu = upper_half(activations, own, raw)
    *pair, bands = link((early_high, early_low), late, (upper_high, upper_low), uu)
    bands, traces = lax.optimization_barrier((bands, traces))
    parts = lax.all_gather(bands, "row")
    return final(float(entry_count), parts, traces, pair)


def solution(mesh):
    return jax.shard_map(
        body,
        mesh=mesh,
        in_specs=(P("row", "pair"),),
        out_specs=P("row", "pair"),
        check_vma=False,
    )
```

```python
import functools

import jax
import jax.numpy as jnp
from jax import lax
from jax.experimental import pallas as pl
from jax.experimental.pallas import tpu as pltpu
from jax.sharding import PartitionSpec as P

STEPS = 16
BLK = 128
BAND = 16
ROWS = 4 * BAND
TILE = 1024
EARLY = 1056
PART = 256
LIMIT = 24 << 20
COST = pl.CostEstimate(flops=2_000_000_000, bytes_accessed=6_000_000, transcendentals=0)
F32 = jnp.float32
BF16 = jnp.bfloat16


def split(value):
    high = value.astype(BF16)
    return high, (value - high.astype(F32)).astype(BF16)


def mm(left, right, dims):
    return lax.dot_general(left, right, (dims, ((), ())), preferred_element_type=F32)


def gram_tile(tile):
    high, low = split(tile)
    rows = ((0,), (0,))
    cross = mm(high, low, rows)
    return mm(high, high, rows) + mm(low, low, rows) + (cross + cross.T)


def take_band(block, width):
    turned = jnp.concatenate(
        [
            pltpu.roll(block[first : first + 8], (width - 8 - first) % BLK, 1)
            for first in range(0, BLK, 8)
        ],
        axis=0,
    )
    left = 7 - lax.broadcasted_iota(jnp.int32, (BLK, BLK), 0) % 8
    for shift in (1, 2, 4):
        turned = jnp.where(left & shift != 0, pltpu.roll(turned, shift, 1), turned)
    return turned.T[:width, :]


def bands_of(block, width):
    band = take_band(block, width)
    return [band[width - 1 - k : width - k, :] for k in range(width)]


def put_band(band, first):
    padded = jnp.concatenate((band, jnp.zeros((BLK - BAND, BLK), F32)), axis=0)
    return pltpu.roll(padded.T, first % BLK, 1, stride=1, stride_axis=0)


def half_angle(gap, twice):
    gap_size = jnp.abs(gap)
    twice_size = jnp.abs(twice)
    largest = jnp.maximum(gap_size, twice_size)
    scale = jnp.where(largest < 2.0**-20, 2.0**80, 1.0)
    gap_size = jnp.where(largest > 0.0, gap_size * scale, 1.0)
    twice_size = twice_size * scale
    inverse = lax.rsqrt(gap_size * gap_size + twice_size * twice_size)
    half = 0.5 + (0.5 * gap_size) * inverse
    half_inverse = lax.rsqrt(half)
    large = half * half_inverse
    small = (0.5 * twice_size) * inverse * half_inverse
    sign = jnp.where(twice < 0.0, -1.0, 1.0)
    ahead = gap >= 0.0
    return jnp.where(ahead, large, small), sign * jnp.where(ahead, small, large)


def row_copies(rows, index):
    return jnp.broadcast_to(rows[index : index + 1, :], (8, BLK))


def ahead_by_one(rows):
    return pltpu.roll(rows, 1, 1)


def jacobi_bands(uu, ul, lu, ll):
    last = BAND - 1
    is_first = lax.broadcasted_iota(jnp.int32, (BAND, BLK), 0) == 0
    row_ids = lax.broadcasted_iota(jnp.int32, (BAND, BLK), 0)
    one = jnp.where(row_ids == last, 1.0, 0.0).astype(F32)
    zero = jnp.zeros((BAND, BLK), F32)
    u_top, u_low, l_top, l_low = one, zero, zero, one
    u_diag, l_diag, coupling = row_copies(uu, 0), row_copies(ll, 0), row_copies(ul, 0)
    for step in range(STEPS):
        cos, sin = half_angle(u_diag - l_diag, 2.0 * coupling)
        final_step = step == STEPS - 1
        if not final_step:
            u_past, l_past, x_past = (ahead_by_one(v) for v in (u_diag, l_diag, coupling))
            cos_past, sin_past = ahead_by_one(cos), ahead_by_one(sin)
            u_diag, coupling = (
                cos * (cos * u_diag + sin * coupling) + sin * (cos * coupling + sin * l_diag),
                cos_past * (cos * row_copies(ul, 1) + sin * row_copies(ll, 1))
                - sin_past * (cos * row_copies(uu, 1) + sin * row_copies(lu, 1)),
            )
            l_diag = cos_past * (cos_past * l_past - sin_past * x_past) - sin_past * (
                cos_past * x_past - sin_past * u_past
            )
        cos_b = jnp.concatenate([cos] * (BAND // 8), axis=0)
        sin_b = jnp.concatenate([sin] * (BAND // 8), axis=0)
        u_top, l_top = u_top * cos_b + l_top * sin_b, l_top * cos_b - u_top * sin_b
        u_low, l_low = u_low * cos_b + l_low * sin_b, l_low * cos_b - u_low * sin_b
        if final_step:
            break
        cos_d = jnp.concatenate(
            [pltpu.roll(cos, 8 * i, 1, stride=1, stride_axis=0) for i in range(BAND // 8)], axis=0
        )
        sin_d = jnp.concatenate(
            [pltpu.roll(sin, 8 * i, 1, stride=1, stride_axis=0) for i in range(BAND // 8)], axis=0
        )
        uu, lu = uu * cos_b + lu * sin_b, lu * cos_b - uu * sin_b
        ul, ll = ul * cos_b + ll * sin_b, ll * cos_b - ul * sin_b
        uu, ul = uu * cos_d + ul * sin_d, ul * cos_d - uu * sin_d
        lu, ll = lu * cos_d + ll * sin_d, ll * cos_d - lu * sin_d
        ul = pltpu.roll(ul, last, 0)
        lu = jnp.where(is_first, ul, ahead_by_one(pltpu.roll(lu, 1, 0)))
        ll = ahead_by_one(ll)
        l_top = ahead_by_one(pltpu.roll(l_top, last, 0))
        l_low = ahead_by_one(pltpu.roll(l_low, last, 0))
    back = BLK - last
    l_top, l_low = pltpu.roll(l_top, back, 1), pltpu.roll(l_low, back, 1)
    return u_top, u_low, l_top, l_low


def turned_half(top, low, first):
    return jnp.concatenate((put_band(top, first), put_band(low, first)), axis=1)


def times_turned(tile, turned):
    high, low = split(tile)
    turned_high, turned_low = split(turned)
    last = ((1,), (1,))
    return mm(high, turned_high, last) + (mm(high, turned_low, last) + mm(low, turned_high, last))


def all_bands(gram):
    rows = []
    for top in (0, BLK):
        for left in (0, BLK):
            rows += bands_of(gram[top : top + BLK, left : left + BLK], BAND)
    return jnp.concatenate(rows, axis=0)


def summed(parts_ref):
    total = parts_ref[0]
    for i in range(1, parts_ref.shape[0]):
        total = total + parts_ref[i]
    return total


def blocks(bands):
    return [bands[BAND * i : BAND * (i + 1)] for i in range(4)]


VMEM_SPEC = pl.BlockSpec(memory_space=pltpu.VMEM)
PARAMS = pltpu.CompilerParams(vmem_limit_bytes=LIMIT)


def early_kernel(cols_ref, early_ref, sems):
    step = EARLY // sems.shape[0]
    copies = [
        pltpu.make_async_copy(
            cols_ref.at[pl.ds(i * step, step)], early_ref.at[pl.ds(i * step, step)], sems.at[i]
        )
        for i in range(sems.shape[0])
    ]
    for copy in copies:
        copy.start()
    for copy in copies:
        copy.wait()


def early_rows(cols):
    return pl.pallas_call(
        early_kernel,
        in_specs=[pl.BlockSpec(memory_space=pltpu.HBM)],
        out_specs=VMEM_SPEC,
        out_shape=pltpu.VMEM((EARLY, 2 * BLK), F32),
        scratch_shapes=[pltpu.SemaphoreType.DMA((6,))],
        name="early_rows",
    )(cols)


def gram_kernel(cols_ref, bands_ref):
    bands_ref[...] = all_bands(gram_tile(cols_ref[...]))


def gram_bands(cols):
    return pl.pallas_call(
        gram_kernel,
        in_specs=[VMEM_SPEC],
        out_shape=jax.ShapeDtypeStruct((ROWS, BLK), F32),
        compiler_params=PARAMS,
        name="gram_bands",
    )(cols)


def jacobi_kernel(parts_ref, cols_ref, own_ref, late_ref, trace_ref):
    bands = summed(parts_ref)
    uu, ul, lu, ll = blocks(bands)
    trace_ref[...] = jnp.broadcast_to((uu[:1] + ll[:1])[None], trace_ref.shape)
    u_top, u_low, l_top, l_low = jacobi_bands(uu, ul, lu, ll)
    own_ref[...] = jnp.concatenate((u_top, u_low), axis=0)
    late_ref[: 2 * BAND, :] = jnp.concatenate((l_top, l_low), axis=0)
    late_ref[2 * BAND :, :] = times_turned(cols_ref[EARLY:, :], turned_half(l_top, l_low, 0))


def jacobi(parts, cols, copies):
    return pl.pallas_call(
        jacobi_kernel,
        in_specs=[VMEM_SPEC, VMEM_SPEC],
        out_shape=(
            pltpu.VMEM((2 * BAND, BLK), F32),
            jax.ShapeDtypeStruct((2 * BAND + cols.shape[0] - EARLY, BLK), F32),
            jax.ShapeDtypeStruct((copies, 1, BLK), F32),
        ),
        compiler_params=PARAMS,
        name="jacobi",
    )(parts, cols)


def halves_times_turned(high, low, turned):
    turned_high, turned_low = split(turned)
    last = ((1,), (1,))
    return mm(high, turned_high, last) + (mm(high, turned_low, last) + mm(low, turned_high, last))


def upper_kernel(
    cols_ref, own_ref, raw_ref, upper_high, upper_low, raw_high, raw_low, bands_ref, raw_tiles, sems
):
    count = sems.shape[0]
    step = EARLY // count
    loads = [
        pltpu.make_async_copy(raw_ref.at[pl.ds(i * step, step)], raw_tiles.at[pl.ds(i * step, step)], sems.at[i])
        for i in range(count)
    ]
    for load in loads:
        load.start()
    upper = times_turned(cols_ref[...], turned_half(own_ref[:BAND, :], own_ref[BAND:, :], 1 - BAND))
    high, low = split(upper)
    upper_high[...] = high
    upper_low[...] = low
    rows = ((0,), (0,))
    cross = mm(high, low, rows)
    gram = mm(high, high, rows) + mm(low, low, rows) + (cross + cross.T)
    bands_ref[...] = jnp.concatenate(bands_of(gram, BAND), axis=0)
    for load in loads:
        load.wait()
    high, low = split(raw_tiles[...])
    raw_high[...] = high
    raw_low[...] = low


def upper_half(cols, own, raw):
    rows = cols.shape[0]
    upper = jax.ShapeDtypeStruct((rows, BLK), BF16)
    early = jax.ShapeDtypeStruct(raw.shape, BF16)
    return pl.pallas_call(
        upper_kernel,
        in_specs=[VMEM_SPEC, VMEM_SPEC, pl.BlockSpec(memory_space=pltpu.HBM)],
        out_shape=(upper, upper, early, early, jax.ShapeDtypeStruct((BAND, BLK), F32)),
        scratch_shapes=[pltpu.VMEM(raw.shape, F32), pltpu.SemaphoreType.DMA((2,))],
        cost_estimate=COST,
        compiler_params=PARAMS,
        name="upper_half",
    )(cols, own, raw)


def link_kernel(raw_high, raw_low, late_ref, upper_high, upper_low, uu_ref, pair_high, pair_low, bands_ref):
    turned = turned_half(late_ref[:BAND, :], late_ref[BAND : 2 * BAND, :], 0)
    early_high, early_low = split(halves_times_turned(raw_high[...], raw_low[...], turned))
    late_high, late_low = split(late_ref[2 * BAND :, :])
    pair_high[:, :BLK] = upper_high[...]
    pair_low[:, :BLK] = upper_low[...]
    pair_high[:EARLY, BLK:] = early_high
    pair_low[:EARLY, BLK:] = early_low
    pair_high[EARLY:, BLK:] = late_high
    pair_low[EARLY:, BLK:] = late_low
    high, low = pair_high[...], pair_low[...]
    lower_high, lower_low = high[:, BLK:], low[:, BLK:]
    rows = ((0,), (0,))
    gram = (
        mm(lower_high, high, rows)
        + mm(lower_low, low, rows)
        + (mm(lower_high, low, rows) + mm(lower_low, high, rows))
    )
    lu, ll = gram[:, :BLK], gram[:, BLK:]
    bands_ref[:BAND, :] = uu_ref[...]
    bands_ref[BAND:, :] = jnp.concatenate(
        bands_of(lu.T, BAND) + bands_of(lu, BAND) + bands_of(ll, BAND), axis=0
    )


def link(early, late, upper, uu):
    rows = upper[0].shape[0]
    pair = jax.ShapeDtypeStruct((rows, 2 * BLK), BF16)
    return pl.pallas_call(
        link_kernel,
        in_specs=[VMEM_SPEC] * 6,
        out_shape=(pair, pair, jax.ShapeDtypeStruct((ROWS, BLK), F32)),
        cost_estimate=COST,
        compiler_params=PARAMS,
        name="link",
    )(*early, late, *upper, uu)


def final_kernel(
    entry_count, parts_ref, traces_ref, pair_high, pair_low, out_ref, tiles_ref, high_ref, low_ref, sems
):
    rms = jnp.sqrt(jnp.sum(summed(traces_ref), axis=1, keepdims=True) / entry_count)
    u_top, u_low, l_top, l_low = jacobi_bands(*blocks(summed(parts_ref)))
    for first, turned in (
        (0, turned_half(u_top, u_low, 1 - BAND)),
        (BLK, turned_half(l_top, l_low, 0)),
    ):
        high, low = split(turned / rms)
        high_ref[first : first + BLK, :] = high
        low_ref[first : first + BLK, :] = low
    last = ((1,), (1,))
    stores = []
    for i in range(tiles_ref.shape[0]):
        rows = pl.ds(i * PART, PART)
        high, low = pair_high[rows, :], pair_low[rows, :]
        tiles_ref[i] = mm(high, high_ref[...], last) + (
            mm(high, low_ref[...], last) + mm(low, high_ref[...], last)
        )
        store = pltpu.make_async_copy(tiles_ref.at[i], out_ref.at[rows], sems.at[i])
        store.start()
        stores.append(store)
    for store in stores:
        store.wait()


def final(entry_count, parts, traces, pair):
    rows = pair[0].shape[0]
    count = rows // PART
    return pl.pallas_call(
        functools.partial(final_kernel, entry_count),
        in_specs=[VMEM_SPEC] * 4,
        out_specs=pl.BlockSpec(memory_space=pltpu.HBM),
        out_shape=jax.ShapeDtypeStruct((rows, 2 * BLK), F32),
        scratch_shapes=[
            pltpu.VMEM((count, PART, 2 * BLK), F32),
            pltpu.VMEM((2 * BLK, 2 * BLK), BF16),
            pltpu.VMEM((2 * BLK, 2 * BLK), BF16),
            pltpu.SemaphoreType.DMA((count,)),
        ],
        compiler_params=PARAMS,
        name="final",
    )(parts, traces, *pair)


def to_next(value):
    count = lax.axis_size("pair")
    return lax.ppermute(value, "pair", [(pair, (pair + 1) % count) for pair in range(count)])


def body(activations):
    pairs, rows = lax.axis_size("pair"), lax.axis_size("row")
    entry_count = activations.shape[0] * activations.shape[1] * pairs * rows

    raw = to_next(early_rows(activations))
    bands = gram_bands(activations)
    own, late, traces = jacobi(lax.all_gather(bands, "row"), activations, pairs)
    late = to_next(late)
    traces = lax.all_to_all(traces, "pair", 0, 0, tiled=True)
    upper_high, upper_low, early_high, early_low, uu = upper_half(activations, own, raw)
    *pair, bands = link((early_high, early_low), late, (upper_high, upper_low), uu)
    bands, traces = lax.optimization_barrier((bands, traces))
    parts = lax.all_gather(bands, "row")
    return final(float(entry_count), parts, traces, pair)


def solution(mesh):
    return jax.shard_map(
        body,
        mesh=mesh,
        in_specs=(P("row", "pair"),),
        out_specs=P("row", "pair"),
        check_vma=False,
    )
```

```python
import functools

import jax
import jax.numpy as jnp
from jax import lax
from jax.experimental import pallas as pl
from jax.experimental.pallas import tpu as pltpu
from jax.sharding import PartitionSpec as P

STEPS = 16
BLK = 128
BAND = 16
ROWS = 4 * BAND
TILE = 1024
EARLY = 1088
PART = 256
LIMIT = 24 << 20
COST = pl.CostEstimate(flops=2_000_000_000, bytes_accessed=6_000_000, transcendentals=0)
F32 = jnp.float32
BF16 = jnp.bfloat16


def split(value):
    high = value.astype(BF16)
    return high, (value - high.astype(F32)).astype(BF16)


def mm(left, right, dims):
    return lax.dot_general(left, right, (dims, ((), ())), preferred_element_type=F32)


def gram_tile(tile):
    high, low = split(tile)
    rows = ((0,), (0,))
    cross = mm(high, low, rows)
    return mm(high, high, rows) + mm(low, low, rows) + (cross + cross.T)


def take_band(block, width):
    turned = jnp.concatenate(
        [
            pltpu.roll(block[first : first + 8], (width - 8 - first) % BLK, 1)
            for first in range(0, BLK, 8)
        ],
        axis=0,
    )
    left = 7 - lax.broadcasted_iota(jnp.int32, (BLK, BLK), 0) % 8
    for shift in (1, 2, 4):
        turned = jnp.where(left & shift != 0, pltpu.roll(turned, shift, 1), turned)
    return turned.T[:width, :]


def bands_of(block, width):
    band = take_band(block, width)
    return [band[width - 1 - k : width - k, :] for k in range(width)]


def put_band(band, first):
    padded = jnp.concatenate((band, jnp.zeros((BLK - BAND, BLK), F32)), axis=0)
    return pltpu.roll(padded.T, first % BLK, 1, stride=1, stride_axis=0)


def half_angle(gap, twice):
    gap_size = jnp.abs(gap)
    twice_size = jnp.abs(twice)
    largest = jnp.maximum(gap_size, twice_size)
    scale = jnp.where(largest < 2.0**-20, 2.0**80, 1.0)
    gap_size = jnp.where(largest > 0.0, gap_size * scale, 1.0)
    twice_size = twice_size * scale
    inverse = lax.rsqrt(gap_size * gap_size + twice_size * twice_size)
    half = 0.5 + (0.5 * gap_size) * inverse
    half_inverse = lax.rsqrt(half)
    large = half * half_inverse
    small = (0.5 * twice_size) * inverse * half_inverse
    sign = jnp.where(twice < 0.0, -1.0, 1.0)
    ahead = gap >= 0.0
    return jnp.where(ahead, large, small), sign * jnp.where(ahead, small, large)


def row_copies(rows, index):
    return jnp.broadcast_to(rows[index : index + 1, :], (8, BLK))


def ahead_by_one(rows):
    return pltpu.roll(rows, 1, 1)


def jacobi_bands(uu, ul, lu, ll):
    last = BAND - 1
    is_first = lax.broadcasted_iota(jnp.int32, (BAND, BLK), 0) == 0
    row_ids = lax.broadcasted_iota(jnp.int32, (BAND, BLK), 0)
    one = jnp.where(row_ids == last, 1.0, 0.0).astype(F32)
    zero = jnp.zeros((BAND, BLK), F32)
    u_top, u_low, l_top, l_low = one, zero, zero, one
    u_diag, l_diag, coupling = row_copies(uu, 0), row_copies(ll, 0), row_copies(ul, 0)
    for step in range(STEPS):
        cos, sin = half_angle(u_diag - l_diag, 2.0 * coupling)
        final_step = step == STEPS - 1
        if not final_step:
            u_past, l_past, x_past = (ahead_by_one(v) for v in (u_diag, l_diag, coupling))
            cos_past, sin_past = ahead_by_one(cos), ahead_by_one(sin)
            u_diag, coupling = (
                cos * (cos * u_diag + sin * coupling) + sin * (cos * coupling + sin * l_diag),
                cos_past * (cos * row_copies(ul, 1) + sin * row_copies(ll, 1))
                - sin_past * (cos * row_copies(uu, 1) + sin * row_copies(lu, 1)),
            )
            l_diag = cos_past * (cos_past * l_past - sin_past * x_past) - sin_past * (
                cos_past * x_past - sin_past * u_past
            )
        cos_b = jnp.concatenate([cos] * (BAND // 8), axis=0)
        sin_b = jnp.concatenate([sin] * (BAND // 8), axis=0)
        u_top, l_top = u_top * cos_b + l_top * sin_b, l_top * cos_b - u_top * sin_b
        u_low, l_low = u_low * cos_b + l_low * sin_b, l_low * cos_b - u_low * sin_b
        if final_step:
            break
        cos_d = jnp.concatenate(
            [pltpu.roll(cos, 8 * i, 1, stride=1, stride_axis=0) for i in range(BAND // 8)], axis=0
        )
        sin_d = jnp.concatenate(
            [pltpu.roll(sin, 8 * i, 1, stride=1, stride_axis=0) for i in range(BAND // 8)], axis=0
        )
        uu, lu = uu * cos_b + lu * sin_b, lu * cos_b - uu * sin_b
        ul, ll = ul * cos_b + ll * sin_b, ll * cos_b - ul * sin_b
        uu, ul = uu * cos_d + ul * sin_d, ul * cos_d - uu * sin_d
        lu, ll = lu * cos_d + ll * sin_d, ll * cos_d - lu * sin_d
        ul = pltpu.roll(ul, last, 0)
        lu = jnp.where(is_first, ul, ahead_by_one(pltpu.roll(lu, 1, 0)))
        ll = ahead_by_one(ll)
        l_top = ahead_by_one(pltpu.roll(l_top, last, 0))
        l_low = ahead_by_one(pltpu.roll(l_low, last, 0))
    back = BLK - last
    l_top, l_low = pltpu.roll(l_top, back, 1), pltpu.roll(l_low, back, 1)
    return u_top, u_low, l_top, l_low


def turned_half(top, low, first):
    return jnp.concatenate((put_band(top, first), put_band(low, first)), axis=1)


def times_turned(tile, turned):
    high, low = split(tile)
    turned_high, turned_low = split(turned)
    last = ((1,), (1,))
    return mm(high, turned_high, last) + (mm(high, turned_low, last) + mm(low, turned_high, last))


def all_bands(gram):
    rows = []
    for top in (0, BLK):
        for left in (0, BLK):
            rows += bands_of(gram[top : top + BLK, left : left + BLK], BAND)
    return jnp.concatenate(rows, axis=0)


def summed(parts_ref):
    total = parts_ref[0]
    for i in range(1, parts_ref.shape[0]):
        total = total + parts_ref[i]
    return total


def blocks(bands):
    return [bands[BAND * i : BAND * (i + 1)] for i in range(4)]


VMEM_SPEC = pl.BlockSpec(memory_space=pltpu.VMEM)
PARAMS = pltpu.CompilerParams(vmem_limit_bytes=LIMIT)


def early_kernel(cols_ref, early_ref, sems):
    step = EARLY // sems.shape[0]
    copies = [
        pltpu.make_async_copy(
            cols_ref.at[pl.ds(i * step, step)], early_ref.at[pl.ds(i * step, step)], sems.at[i]
        )
        for i in range(sems.shape[0])
    ]
    for copy in copies:
        copy.start()
    for copy in copies:
        copy.wait()


def early_rows(cols):
    return pl.pallas_call(
        early_kernel,
        in_specs=[pl.BlockSpec(memory_space=pltpu.HBM)],
        out_specs=VMEM_SPEC,
        out_shape=pltpu.VMEM((EARLY, 2 * BLK), F32),
        scratch_shapes=[pltpu.SemaphoreType.DMA((4,))],
        name="early_rows",
    )(cols)


def gram_kernel(cols_ref, bands_ref):
    bands_ref[...] = all_bands(gram_tile(cols_ref[...]))


def gram_bands(cols):
    return pl.pallas_call(
        gram_kernel,
        in_specs=[VMEM_SPEC],
        out_shape=jax.ShapeDtypeStruct((ROWS, BLK), F32),
        compiler_params=PARAMS,
        name="gram_bands",
    )(cols)


def jacobi_kernel(parts_ref, cols_ref, own_ref, late_ref, trace_ref):
    bands = summed(parts_ref)
    uu, ul, lu, ll = blocks(bands)
    trace_ref[...] = jnp.broadcast_to((uu[:1] + ll[:1])[None], trace_ref.shape)
    u_top, u_low, l_top, l_low = jacobi_bands(uu, ul, lu, ll)
    own_ref[...] = jnp.concatenate((u_top, u_low), axis=0)
    late_ref[: 2 * BAND, :] = jnp.concatenate((l_top, l_low), axis=0)
    late_ref[2 * BAND :, :] = times_turned(cols_ref[EARLY:, :], turned_half(l_top, l_low, 0))


def jacobi(parts, cols, copies):
    return pl.pallas_call(
        jacobi_kernel,
        in_specs=[VMEM_SPEC, VMEM_SPEC],
        out_shape=(
            pltpu.VMEM((2 * BAND, BLK), F32),
            jax.ShapeDtypeStruct((2 * BAND + cols.shape[0] - EARLY, BLK), F32),
            jax.ShapeDtypeStruct((copies, 1, BLK), F32),
        ),
        compiler_params=PARAMS,
        name="jacobi",
    )(parts, cols)


def halves_times_turned(high, low, turned):
    turned_high, turned_low = split(turned)
    last = ((1,), (1,))
    return mm(high, turned_high, last) + (mm(high, turned_low, last) + mm(low, turned_high, last))


def upper_kernel(
    cols_ref, own_ref, raw_ref, upper_high, upper_low, raw_high, raw_low, bands_ref, raw_tiles, sems
):
    count = sems.shape[0]
    step = EARLY // count
    loads = [
        pltpu.make_async_copy(raw_ref.at[pl.ds(i * step, step)], raw_tiles.at[pl.ds(i * step, step)], sems.at[i])
        for i in range(count)
    ]
    for load in loads:
        load.start()
    upper = times_turned(cols_ref[...], turned_half(own_ref[:BAND, :], own_ref[BAND:, :], 1 - BAND))
    high, low = split(upper)
    upper_high[...] = high
    upper_low[...] = low
    rows = ((0,), (0,))
    cross = mm(high, low, rows)
    gram = mm(high, high, rows) + mm(low, low, rows) + (cross + cross.T)
    bands_ref[...] = jnp.concatenate(bands_of(gram, BAND), axis=0)
    for load in loads:
        load.wait()
    high, low = split(raw_tiles[...])
    raw_high[...] = high
    raw_low[...] = low


def upper_half(cols, own, raw):
    rows = cols.shape[0]
    upper = jax.ShapeDtypeStruct((rows, BLK), BF16)
    early = jax.ShapeDtypeStruct(raw.shape, BF16)
    return pl.pallas_call(
        upper_kernel,
        in_specs=[VMEM_SPEC, VMEM_SPEC, pl.BlockSpec(memory_space=pltpu.HBM)],
        out_shape=(upper, upper, early, early, jax.ShapeDtypeStruct((BAND, BLK), F32)),
        scratch_shapes=[pltpu.VMEM(raw.shape, F32), pltpu.SemaphoreType.DMA((2,))],
        cost_estimate=COST,
        compiler_params=PARAMS,
        name="upper_half",
    )(cols, own, raw)


def link_kernel(
    raw_high, raw_low, late_ref, upper_high, upper_low, uu_ref, pair_high, pair_low, bands_ref, late_tiles, sems
):
    loads = []
    for i, (first, size) in enumerate(((0, 2 * BAND), (2 * BAND, late_ref.shape[0] - 2 * BAND))):
        rows = pl.ds(first, size)
        load = pltpu.make_async_copy(late_ref.at[rows], late_tiles.at[rows], sems.at[i])
        load.start()
        loads.append(load)
    pair_high[:, :BLK] = upper_high[...]
    pair_low[:, :BLK] = upper_low[...]
    loads[0].wait()
    turned = turned_half(late_tiles[:BAND, :], late_tiles[BAND : 2 * BAND, :], 0)
    early_high, early_low = split(halves_times_turned(raw_high[...], raw_low[...], turned))
    loads[1].wait()
    late_high, late_low = split(late_tiles[2 * BAND :, :])
    pair_high[:EARLY, BLK:] = early_high
    pair_low[:EARLY, BLK:] = early_low
    pair_high[EARLY:, BLK:] = late_high
    pair_low[EARLY:, BLK:] = late_low
    high, low = pair_high[...], pair_low[...]
    lower_high, lower_low = high[:, BLK:], low[:, BLK:]
    rows = ((0,), (0,))
    gram = (
        mm(lower_high, high, rows)
        + mm(lower_low, low, rows)
        + (mm(lower_high, low, rows) + mm(lower_low, high, rows))
    )
    lu, ll = gram[:, :BLK], gram[:, BLK:]
    bands_ref[:BAND, :] = uu_ref[...]
    bands_ref[BAND:, :] = jnp.concatenate(
        bands_of(lu.T, BAND) + bands_of(lu, BAND) + bands_of(ll, BAND), axis=0
    )


def link(early, late, upper, uu):
    rows = upper[0].shape[0]
    pair = jax.ShapeDtypeStruct((rows, 2 * BLK), BF16)
    return pl.pallas_call(
        link_kernel,
        in_specs=[VMEM_SPEC] * 2 + [pl.BlockSpec(memory_space=pltpu.HBM)] + [VMEM_SPEC] * 3,
        out_shape=(pair, pair, jax.ShapeDtypeStruct((ROWS, BLK), F32)),
        scratch_shapes=[pltpu.VMEM(late.shape, F32), pltpu.SemaphoreType.DMA((2,))],
        cost_estimate=COST,
        compiler_params=PARAMS,
        name="link",
    )(*early, late, *upper, uu)


def final_kernel(
    entry_count, parts_ref, traces_ref, pair_high, pair_low, out_ref, tiles_ref, high_ref, low_ref, sems
):
    rms = jnp.sqrt(jnp.sum(summed(traces_ref), axis=1, keepdims=True) / entry_count)
    u_top, u_low, l_top, l_low = jacobi_bands(*blocks(summed(parts_ref)))
    for first, turned in (
        (0, turned_half(u_top, u_low, 1 - BAND)),
        (BLK, turned_half(l_top, l_low, 0)),
    ):
        high, low = split(turned / rms)
        high_ref[first : first + BLK, :] = high
        low_ref[first : first + BLK, :] = low
    last = ((1,), (1,))
    stores = []
    for i in range(tiles_ref.shape[0]):
        rows = pl.ds(i * PART, PART)
        high, low = pair_high[rows, :], pair_low[rows, :]
        tiles_ref[i] = mm(high, high_ref[...], last) + (
            mm(high, low_ref[...], last) + mm(low, high_ref[...], last)
        )
        store = pltpu.make_async_copy(tiles_ref.at[i], out_ref.at[rows], sems.at[i])
        store.start()
        stores.append(store)
    for store in stores:
        store.wait()


def final(entry_count, parts, traces, pair):
    rows = pair[0].shape[0]
    count = rows // PART
    return pl.pallas_call(
        functools.partial(final_kernel, entry_count),
        in_specs=[VMEM_SPEC] * 4,
        out_specs=pl.BlockSpec(memory_space=pltpu.HBM),
        out_shape=jax.ShapeDtypeStruct((rows, 2 * BLK), F32),
        scratch_shapes=[
            pltpu.VMEM((count, PART, 2 * BLK), F32),
            pltpu.VMEM((2 * BLK, 2 * BLK), BF16),
            pltpu.VMEM((2 * BLK, 2 * BLK), BF16),
            pltpu.SemaphoreType.DMA((count,)),
        ],
        compiler_params=PARAMS,
        name="final",
    )(parts, traces, *pair)


def to_next(value):
    count = lax.axis_size("pair")
    return lax.ppermute(value, "pair", [(pair, (pair + 1) % count) for pair in range(count)])


def body(activations):
    pairs, rows = lax.axis_size("pair"), lax.axis_size("row")
    entry_count = activations.shape[0] * activations.shape[1] * pairs * rows

    raw = to_next(early_rows(activations))
    bands = gram_bands(activations)
    own, late, traces = jacobi(lax.all_gather(bands, "row"), activations, pairs)
    late = to_next(late)
    traces = lax.all_to_all(traces, "pair", 0, 0, tiled=True)
    upper_high, upper_low, early_high, early_low, uu = upper_half(activations, own, raw)
    *pair, bands = link((early_high, early_low), late, (upper_high, upper_low), uu)
    bands, traces = lax.optimization_barrier((bands, traces))
    parts = lax.all_gather(bands, "row")
    return final(float(entry_count), parts, traces, pair)


def solution(mesh):
    return jax.shard_map(
        body,
        mesh=mesh,
        in_specs=(P("row", "pair"),),
        out_specs=P("row", "pair"),
        check_vma=False,
    )
```
